128 devices in a mesh: phase: 2 (over core), dp: 32 (over z, y, x_lo), mp: 2 (over x_hi).
Axes of the slice: x: 4 (x_hi: 2, x_lo: 2; x = x_hi * 2 + x_lo), y: 4, z: 4, core: 2. Of those that a mesh axis runs over, the one named last changes fastest.
Arguments:
- segments: bfloat16 [2, 64, 64, 4096], P(None, 'dp', 'mp'), may hold values from -6 to 6
- memory_in: bfloat16 [64, 64, 4096], P('dp', 'mp'), may hold values from -6 to 6
- seg_lengths: int32 [2, 64], P(None, 'dp'), may hold values from 1 to 64, as said below
- routes: int32 [2, 32], replicated, may hold values from 0 to 31, each once within a row
- w_query: bfloat16 [2, 4096, 4096], P('phase', None, 'mp'), may hold values from -12 to 12
- w_key: bfloat16 [2, 4096, 1024], P('phase', None, 'mp'), may hold values from -1 to 1
- value_weight: bfloat16 [2, 4096, 1024], P('phase', None, 'mp'), may hold values from -0.09375 to 0.09375
- w_out: bfloat16 [2, 4096, 4096], P('phase', 'mp'), may hold values from -0.09375 to 0.09375
- norm_gain: bfloat16 [2, 4096], P('phase'), may hold values from 0.099609375 to 1.8984375
Outputs:
- mem_states: bfloat16 [2, 2, 64, 64, 4096], P('phase', None, 'dp', 'mp')
- seg_states: bfloat16 [2, 2, 64, 64, 4096], P('phase', None, 'dp', 'mp')
The draws below stay inside these ranges and needn't reach their ends.
Inputs may be any that keep to these rules, and one draw needn't show every extreme that they name: Each row m is a permutation of the data groups: slot m of group g hands its memory to slot m of group routes[m, g]. `seg_lengths`: some entry equals 64.
All inputs are finite; a program needn't handle non-finite values.
Results may differ from the reference program's by a relative error of at most 0.025.
Values may be sent and summed in bfloat16 or wider, within the bound.
A program may use at most 192 MiB of HBM per device.

```python
from functools import partial
import jax
import jax.numpy as jnp
from jax import lax

MODEL_WIDTH = 4096
QUERY_HEADS = 32
KEY_VALUE_HEADS = 8
HEAD_SIZE = 128
MEM = 64
SEG = 64
ROUNDS = 2
MB = 2
SLOTS = 64
N_PHASE = 2
N_DP = 32
N_MP = 2


def paired_weights(key):
    leading_key, second_key = jax.random.split(jax.random.fold_in(key, 11), 2)
    fanin_scale = MODEL_WIDTH ** (-0.5)
    key_matrices = jnp.clip(jax.random.normal(leading_key, (N_PHASE, MODEL_WIDTH, KEY_VALUE_HEADS * HEAD_SIZE), jnp.float32), -6.0, 6.0) * fanin_scale
    drawn_query = jnp.clip(jax.random.normal(second_key, (N_PHASE, MODEL_WIDTH, QUERY_HEADS * HEAD_SIZE), jnp.float32), -6.0, 6.0) * fanin_scale
    return (key_matrices, drawn_query)


def draw_w_key(key, part):
    key_matrices, drawn_query = paired_weights(key)
    return key_matrices.astype(jnp.bfloat16)


def draw_w_query(key, part):
    key_matrices, drawn_query = paired_weights(key)
    return drawn_query.astype(jnp.bfloat16)


def draw_seg_lengths(key, part):
    leading_key, second_key = jax.random.split(jax.random.fold_in(key, 23), 2)
    lengths = jax.random.randint(leading_key, (ROUNDS * SLOTS,), 1, SEG + 1)
    full_spot = jax.random.randint(second_key, (), 0, ROUNDS * SLOTS)
    lengths = jnp.where(jnp.arange(ROUNDS * SLOTS) == full_spot, SEG, lengths)
    return lengths.reshape(ROUNDS, SLOTS).astype(jnp.int32)


def steps_of(stream_key, dims, pieces, smallest, top_value):
    factor_of, own = 1.0, jax.random.fold_in(stream_key, 6)
    for dim, parts in pieces:
        heights = jnp.exp(jax.random.uniform(jax.random.fold_in(own, dim), (parts,), jnp.float32, smallest / len(pieces), top_value / len(pieces)))
        factor_of = factor_of * jnp.repeat(heights, dims[dim] // parts).reshape([-1 if axis == dim else 1 for axis in range(len(dims))])
    return factor_of


def normal_values(stream_key, extent, spread, limit, pieces=(), held_as=jnp.bfloat16):
    array = spread * jax.random.normal(stream_key, extent, jnp.float32)
    if pieces:
        array = array * steps_of(stream_key, extent, pieces, -0.22, 0.18)
    return jnp.clip(array, -limit, limit).astype(held_as)


def setup_inputs(seed: int = 0) -> dict:
    arg_keys = jax.random.split(jax.random.key(seed), 10)
    segments = normal_values(arg_keys[0], (ROUNDS, SLOTS, SEG, MODEL_WIDTH), 1.0, 6.0, ((1, 32), (2, 2)))
    memory_in = normal_values(arg_keys[1], (SLOTS, MEM, MODEL_WIDTH), 1.0, 6.0, ((0, 32), (1, 2)))
    seg_lengths = draw_seg_lengths(jax.random.fold_in(arg_keys[9], 71), 0)
    routes = jax.vmap(lambda own: jax.random.permutation(own, N_DP))(jax.random.split(arg_keys[3], MB)).reshape((MB, N_DP)).astype(jnp.int32)
    w_query = draw_w_query(jax.random.fold_in(arg_keys[9], 71), 0)
    w_key = draw_w_key(jax.random.fold_in(arg_keys[9], 71), 0)
    value_weight = normal_values(arg_keys[6], (N_PHASE, MODEL_WIDTH, KEY_VALUE_HEADS * HEAD_SIZE), MODEL_WIDTH ** -0.5, 0.09375, ((0, 2), (2, 2)))
    w_out = normal_values(arg_keys[7], (N_PHASE, QUERY_HEADS * HEAD_SIZE, MODEL_WIDTH), (QUERY_HEADS * HEAD_SIZE) ** -0.5, 0.09375, ((0, 2), (1, 2)))
    norm_gain = jnp.clip(1.0 + 0.18 * jax.random.normal(arg_keys[8], (N_PHASE, MODEL_WIDTH), jnp.float32), 0.099609375, 1.8984375).astype(jnp.bfloat16)
    return dict(segments=segments, memory_in=memory_in, seg_lengths=seg_lengths, routes=routes, w_query=w_query, w_key=w_key, value_weight=value_weight, w_out=w_out, norm_gain=norm_gain)


EPSILON = 1e-05

def norm_rows(rows, gain):
    values = rows.astype(jnp.float32)
    scaled = values * lax.rsqrt(lax.optimization_barrier(jnp.mean(values * values, axis=-1, keepdims=True)) + EPSILON)
    return (scaled * gain.astype(jnp.float32)).astype(jnp.bfloat16)

def section_layer(mem_x, seg_x, length, w_query, w_key, value_weight, w_out, gain):
    combined = jnp.concatenate([mem_x, seg_x], axis=0)
    rows_total = combined.shape[0]
    normed = norm_rows(combined, gain)
    query_rows = jnp.dot(normed, w_query, preferred_element_type=jnp.float32).astype(jnp.bfloat16)
    rows_of_key = jnp.dot(normed, w_key, preferred_element_type=jnp.float32).astype(jnp.bfloat16)
    rows_of_value = jnp.dot(normed, value_weight, preferred_element_type=jnp.float32).astype(jnp.bfloat16)
    heads_of_query = query_rows.astype(jnp.float32).reshape(rows_total, KEY_VALUE_HEADS, QUERY_HEADS // KEY_VALUE_HEADS, HEAD_SIZE)
    heads_of_key = rows_of_key.astype(jnp.float32).reshape(rows_total, KEY_VALUE_HEADS, HEAD_SIZE)
    heads_of_value = rows_of_value.astype(jnp.float32).reshape(rows_total, KEY_VALUE_HEADS, HEAD_SIZE)
    scores = jnp.einsum('qcgd,kcd->cgqk', heads_of_query, heads_of_key) * HEAD_SIZE ** (-0.5)
    position = jnp.arange(rows_total, dtype=jnp.int32)
    query_pos = position[:, None]
    key_pos = position[None, :]
    visible = (key_pos < MEM) | (key_pos - MEM < length) & ((query_pos < MEM) | (key_pos <= query_pos))
    scores = jnp.where(visible, scores, -1e+30)
    row_max = lax.optimization_barrier(jnp.max(scores, axis=-1, keepdims=True))
    exponent = jnp.exp(scores - row_max)
    attn = (exponent / lax.optimization_barrier(jnp.sum(exponent, axis=-1, keepdims=True))).astype(jnp.bfloat16)
    attended = jnp.einsum('cgqk,kcd->qcgd', attn.astype(jnp.float32), heads_of_value)
    attended = attended.astype(jnp.bfloat16).reshape(rows_total, QUERY_HEADS * HEAD_SIZE)
    group_cols = QUERY_HEADS * HEAD_SIZE // N_MP
    head_sum = jnp.zeros((rows_total, MODEL_WIDTH), jnp.float32)
    for column_group in range(N_MP):
        lower = column_group * group_cols
        term = jnp.dot(attended[:, lower:lower + group_cols], w_out[lower:lower + group_cols], preferred_element_type=jnp.float32).astype(jnp.bfloat16)
        term = lax.optimization_barrier(term)
        head_sum = head_sum + term.astype(jnp.float32)
    layer_out = (combined.astype(jnp.float32) + head_sum).astype(jnp.bfloat16)
    return (layer_out[:MEM], layer_out[MEM:])

def run_section(packed, weights):
    return section_layer(packed[0], packed[1], packed[2], weights[0], weights[1], weights[2], weights[3], weights[4])

def reference(segments, memory_in, seg_lengths, routes, w_query, w_key, value_weight, w_out, norm_gain):
    memory = memory_in
    mem_record = [[] for section in range(N_PHASE)]
    seg_record = [[] for section in range(N_PHASE)]
    for round_index in range(ROUNDS):
        mem_rows = memory
        seg_rows = segments[round_index]
        for section in range(N_PHASE):
            weights = (w_query[section], w_key[section], value_weight[section], w_out[section], norm_gain[section])
            mem_rows, seg_rows = lax.map(partial(run_section, weights=weights), (mem_rows, seg_rows, seg_lengths[round_index]))
            mem_record[section].append(mem_rows)
            seg_record[section].append(seg_rows)
        if round_index + 1 < ROUNDS:
            source = mem_rows.reshape(N_DP, MB, MEM, MODEL_WIDTH).astype(jnp.float32)
            groups = jnp.arange(N_DP, dtype=jnp.int32)
            selector = (routes[:, None, :] == groups[None, :, None]).astype(jnp.float32)
            routed = jnp.einsum('mdg,gmre->dmre', selector, source, precision=lax.Precision.HIGHEST)
            memory = routed.reshape(N_DP * MB, MEM, MODEL_WIDTH).astype(jnp.bfloat16)
    mem_states = jnp.stack([jnp.stack(mem_record[section], 0) for section in range(N_PHASE)], 0)
    seg_states = jnp.stack([jnp.stack(seg_record[section], 0) for section in range(N_PHASE)], 0)
    return (mem_states, seg_states)
```

```python
import functools

import jax
import jax.numpy as jnp
from jax import lax
from jax.experimental import pallas as pl
from jax.experimental.pallas import tpu as pltpu
from jax.sharding import PartitionSpec as P

HEAD_SIZE = 128
EPSILON = 1e-05
CHUNKS = 4
TILE = 512
MESH = pl.DeviceIdType.MESH


def window_kernel(
    segments, memory, lengths, gain, w_query, w_key, w_value, w_out,
    mem_out, seg_out,
    wq, wk, wv, wo, gathered, rows_home, partial, received, normed, queries, keys, values, attended, far_lengths,
    wq_sem, wk_sem, wv_sem, wo_sem, len_sem, gather_send, gather_recv, home_send, home_recv, sum_send, sum_recv, out_sem,
):
    phase = lax.axis_index("phase")
    group = lax.axis_index("dp")
    half = lax.axis_index("mp")
    across = group + 1 - 2 * (group % 2)
    rounds, slots, dev_rows, width = segments.shape
    block = 2 * dev_rows
    items = rounds * slots
    chunk = width // CHUNKS
    first = phase == 0
    second = phase == 1

    def weight_copies():
        copies = []
        for tile in range(wq.shape[1] // TILE):
            cols = pl.ds(tile * TILE, TILE)
            copies.append(pltpu.make_async_copy(w_query.at[0, :, cols], wq.at[:, cols], wq_sem.at[tile]))
        copies.append(pltpu.make_async_copy(w_key.at[0], wk, wk_sem))
        copies.append(pltpu.make_async_copy(w_value.at[0], wv, wv_sem))
        for tile in range(wo.shape[1] // TILE):
            cols = pl.ds(tile * TILE, TILE)
            copies.append(pltpu.make_async_copy(w_out.at[0, :, cols], wo.at[:, cols], wo_sem.at[tile]))
        return copies

    def length_copy():
        return pltpu.make_async_remote_copy(
            src_ref=lengths, dst_ref=far_lengths, send_sem=len_sem.at[0], recv_sem=len_sem.at[1],
            device_id=(phase, across, half), device_id_type=MESH,
        )

    def input_copies(item):
        rnd, slot = item // slots, item % slots
        sources = (memory.at[slot], segments.at[rnd, slot])
        far, own = [], []
        for kind in range(2):
            for target in range(2):
                far.append(pltpu.make_async_remote_copy(
                    src_ref=sources[kind],
                    dst_ref=gathered.at[item, pl.ds(pl.multiple_of(half * block + kind * dev_rows, dev_rows), dev_rows)],
                    send_sem=gather_send.at[item, target, kind],
                    recv_sem=gather_recv.at[item, half, kind],
                    device_id=(0, across, target), device_id_type=MESH,
                ))
            own.append(pltpu.make_async_copy(
                sources[kind], rows_home.at[item, pl.ds(kind * dev_rows, dev_rows)], home_recv.at[item, kind]))
        return far, own

    def hand_copies(item, index):
        cols = pl.ds(pl.multiple_of(index * chunk, chunk), chunk)
        far = []
        for target in range(2):
            far.append(pltpu.make_async_remote_copy(
                src_ref=rows_home.at[item, :, cols],
                dst_ref=gathered.at[item, pl.ds(pl.multiple_of(half * block, block), block), cols],
                send_sem=gather_send.at[item, target, index],
                recv_sem=gather_recv.at[item, half, index],
                device_id=(1, across, target), device_id_type=MESH,
            ))
        far.append(pltpu.make_async_remote_copy(
            src_ref=rows_home.at[item, :, cols], dst_ref=rows_home.at[item, :, cols],
            send_sem=home_send.at[item, index], recv_sem=home_recv.at[item, index],
            device_id=(1, group, half), device_id_type=MESH,
        ))
        return far

    def sum_copy(item, index, target):
        cols = pl.ds(pl.multiple_of(index * chunk, chunk), chunk)
        return pltpu.make_async_remote_copy(
            src_ref=partial.at[item, pl.ds(target * block, block), cols],
            dst_ref=received.at[item, half, :, cols],
            send_sem=sum_send.at[item, index, target],
            recv_sem=sum_recv.at[item, half, index],
            device_id=(phase, across, target), device_id_type=MESH,
        )

    def out_copies(item):
        rnd, slot = item // slots, item % slots
        return (
            pltpu.make_async_copy(rows_home.at[item, pl.ds(0, dev_rows)], mem_out.at[0, rnd, slot], out_sem.at[item, 0]),
            pltpu.make_async_copy(rows_home.at[item, pl.ds(dev_rows, dev_rows)], seg_out.at[0, rnd, slot], out_sem.at[item, 1]),
        )

    barrier = pltpu.get_barrier_semaphore()
    for target in range(2):
        pl.semaphore_signal(barrier, inc=1, device_id=(phase, across, target), device_id_type=MESH)

    @pl.when(second)
    def _():
        for target in range(2):
            pl.semaphore_signal(barrier, inc=1, device_id=(0, across, target), device_id_type=MESH)
        pl.semaphore_signal(barrier, inc=1, device_id=(0, group, half), device_id_type=MESH)

    for copy in weight_copies():
        copy.start()

    @pl.when(first)
    def _():
        pl.semaphore_wait(barrier, 5)

    @pl.when(second)
    def _():
        pl.semaphore_wait(barrier, 2)

    length_copy().start()

    @pl.when(first)
    def _():
        @pl.loop(0, items)
        def _(item):
            far, own = input_copies(item)
            for copy in far + own:
                copy.start()

    length_copy().wait()

    def positions(axis):
        index = lax.broadcasted_iota(jnp.int32, (2 * block, 2 * block), axis)
        part, within = index // block, index % block
        return jnp.where(within < dev_rows, part * dev_rows + within, block + part * dev_rows + within - dev_rows)

    def compute(item):
        @pl.when(first)
        def _():
            for origin in range(2):
                for kind in range(2):
                    here = gathered.at[item, pl.ds(origin * block + kind * dev_rows, dev_rows)]
                    pltpu.make_async_copy(here, here, gather_recv.at[item, origin, kind]).wait()

        @pl.when(second)
        def _():
            for origin in range(2):
                for index in range(CHUNKS):
                    here = gathered.at[item, pl.ds(origin * block, block), pl.ds(index * chunk, chunk)]
                    pltpu.make_async_copy(here, here, gather_recv.at[item, origin, index]).wait()

        scale_row = gain[...].astype(jnp.float32)

        @pl.loop(0, 2 * block // 16)
        def _(step):
            rows = pl.ds(pl.multiple_of(step * 16, 16), 16)
            x = gathered[item, rows].astype(jnp.float32)
            scaled = x * lax.rsqrt(jnp.mean(x * x, axis=-1, keepdims=True) + EPSILON)
            normed[rows] = (scaled * scale_row).astype(jnp.bfloat16)

        @pl.loop(0, wq.shape[1] // TILE)
        def _(tile):
            cols = pl.ds(pl.multiple_of(tile * TILE, TILE), TILE)

            @pl.when(item == 0)
            def _():
                pltpu.make_async_copy(w_query.at[0, :, cols], wq.at[:, cols], wq_sem.at[tile]).wait()

            queries[:, cols] = jnp.dot(normed[...], wq[:, cols], preferred_element_type=jnp.float32).astype(jnp.bfloat16)

        @pl.when(item == 0)
        def _():
            pltpu.make_async_copy(w_key.at[0], wk, wk_sem).wait()
            pltpu.make_async_copy(w_value.at[0], wv, wv_sem).wait()

        keys[...] = jnp.dot(normed[...], wk[...], preferred_element_type=jnp.float32).astype(jnp.bfloat16)
        values[...] = jnp.dot(normed[...], wv[...], preferred_element_type=jnp.float32).astype(jnp.bfloat16)

        length = far_lengths[pl.ds(item, 1), :]
        query_pos, key_pos = positions(0), positions(1)
        visible = (key_pos < block) | (key_pos - block < length) & ((query_pos < block) | (key_pos <= query_pos))
        heads = wq.shape[1] // HEAD_SIZE
        kv_heads = wk.shape[1] // HEAD_SIZE
        per = heads // kv_heads
        for kv in range(kv_heads):
            k = keys[:, kv * HEAD_SIZE:(kv + 1) * HEAD_SIZE]
            v = values[:, kv * HEAD_SIZE:(kv + 1) * HEAD_SIZE]
            for head in range(kv * per, (kv + 1) * per):
                q = queries[:, head * HEAD_SIZE:(head + 1) * HEAD_SIZE]
                scores = lax.dot_general(q, k, (((1,), (1,)), ((), ())), preferred_element_type=jnp.float32)
                scores = jnp.where(visible, scores * HEAD_SIZE ** (-0.5), -1e30)
                weights = jnp.exp(scores - jnp.max(scores, axis=-1, keepdims=True))
                attn = (weights / jnp.sum(weights, axis=-1, keepdims=True)).astype(jnp.bfloat16)
                attended[:, head * HEAD_SIZE:(head + 1) * HEAD_SIZE] = jnp.dot(
                    attn, v, preferred_element_type=jnp.float32).astype(jnp.bfloat16)

        @pl.loop(0, CHUNKS)
        def _(index):
            for step in range(chunk // TILE):
                tile = index * (chunk // TILE) + step
                cols = pl.ds(pl.multiple_of(tile * TILE, TILE), TILE)

                @pl.when(item == 0)
                def _():
                    pltpu.make_async_copy(w_out.at[0, :, cols], wo.at[:, cols], wo_sem.at[tile]).wait()

                partial[item, :, cols] = jnp.dot(
                    attended[...], wo[:, cols], preferred_element_type=jnp.float32).astype(jnp.bfloat16)
            for target in range(2):
                sum_copy(item, index, target).start()

    def home(item):
        @pl.when(first)
        def _():
            for copy in input_copies(item)[1]:
                copy.wait()

        @pl.loop(0, CHUNKS)
        def _(index):
            cols = pl.ds(pl.multiple_of(index * chunk, chunk), chunk)

            @pl.when(second)
            def _():
                here = rows_home.at[item, :, cols]
                pltpu.make_async_copy(here, here, home_recv.at[item, index]).wait()

            for origin in range(2):
                here = received.at[item, origin, :, cols]
                pltpu.make_async_copy(here, here, sum_recv.at[item, origin, index]).wait()
            total = received[item, 0, :, cols].astype(jnp.float32) + received[item, 1, :, cols].astype(jnp.float32)
            rows_home[item, :, cols] = (rows_home[item, :, cols].astype(jnp.float32) + total).astype(jnp.bfloat16)

            @pl.when(first)
            def _():
                for copy in hand_copies(item, index):
                    copy.start()

        for copy in out_copies(item):
            copy.start()

    @pl.loop(0, items)
    def _(item):
        compute(item)

    @pl.loop(0, items)
    def _(item):
        home(item)

    @pl.loop(0, items)
    def _(item):
        for copy in out_copies(item):
            copy.wait()

        @pl.loop(0, CHUNKS)
        def _(index):
            for target in range(2):
                sum_copy(item, index, target).wait_send()

        @pl.when(first)
        def _():
            for copy in input_copies(item)[0]:
                copy.wait_send()

            @pl.loop(0, CHUNKS)
            def _(index):
                for copy in hand_copies(item, index):
                    copy.wait_send()


def run_window(segments, memory, lengths, gain, w_query, w_key, w_value, w_out):
    rounds, slots, dev_rows, width = segments.shape
    items = rounds * slots
    block = 2 * dev_rows
    rows = 2 * block
    bf16 = jnp.bfloat16
    dma = pltpu.SemaphoreType.DMA
    states = jax.ShapeDtypeStruct((1, rounds, slots, dev_rows, width), bf16)
    return pl.pallas_call(
        window_kernel,
        out_shape=(states, states),
        in_specs=[pl.BlockSpec(memory_space=pl.ANY)] * 2
        + [pl.BlockSpec(memory_space=pltpu.VMEM)] * 2
        + [pl.BlockSpec(memory_space=pl.ANY)] * 4,
        out_specs=(pl.BlockSpec(memory_space=pl.ANY), pl.BlockSpec(memory_space=pl.ANY)),
        scratch_shapes=[
            pltpu.VMEM(w_query.shape[1:], bf16),
            pltpu.VMEM(w_key.shape[1:], bf16),
            pltpu.VMEM(w_value.shape[1:], bf16),
            pltpu.VMEM(w_out.shape[1:], bf16),
            pltpu.VMEM((items, rows, width), bf16),
            pltpu.VMEM((items, block, width), bf16),
            pltpu.VMEM((items, rows, width), bf16),
            pltpu.VMEM((items, 2, block, width), bf16),
            pltpu.VMEM((rows, width), bf16),
            pltpu.VMEM((rows, w_query.shape[2]), bf16),
            pltpu.VMEM((rows, w_key.shape[2]), bf16),
            pltpu.VMEM((rows, w_value.shape[2]), bf16),
            pltpu.VMEM((rows, w_query.shape[2]), bf16),
            pltpu.VMEM(lengths.shape, jnp.int32),
            dma((w_query.shape[2] // TILE,)),
            dma,
            dma,
            dma((width // TILE,)),
            dma((2,)),
            dma((items, 2, CHUNKS)),
            dma((items, 2, CHUNKS)),
            dma((items, CHUNKS)),
            dma((items, CHUNKS)),
            dma((items, CHUNKS, 2)),
            dma((items, 2, CHUNKS)),
            dma((items, 2)),
        ],
        compiler_params=pltpu.CompilerParams(
            collective_id=0, has_side_effects=True, vmem_limit_bytes=60 * 1024 * 1024
        ),
    )(segments, memory, lengths, gain, w_query, w_key, w_value, w_out)


def route_memory(rows, routes):
    slots, dev_rows, width = rows.shape
    groups = routes.shape[1]
    pieces = jnp.moveaxis(rows.reshape(slots, dev_rows, groups, width // groups), 2, 0)
    spread = lax.all_to_all(pieces, "dp", split_axis=0, concat_axis=0, tiled=True)
    ids = jnp.arange(groups, dtype=jnp.int32)
    origin = jnp.sum(jnp.where(routes[:, None, :] == ids[None, :, None], ids[None, None, :], 0), axis=-1)
    picked = jnp.stack([jnp.take(spread[:, slot], origin[slot], axis=0) for slot in range(slots)], axis=1)
    back = lax.all_to_all(picked, "dp", split_axis=0, concat_axis=0, tiled=True)
    return jnp.moveaxis(back, 0, 2).reshape(slots, dev_rows, width)


def per_device(segments, memory_in, seg_lengths, routes, w_query, w_key, value_weight, w_out, norm_gain):
    rounds, slots = segments.shape[:2]
    memory = memory_in
    mem_states, seg_states = [], []
    for rnd in range(rounds):
        lengths = jnp.broadcast_to(jnp.pad(seg_lengths[rnd], (0, 8 - slots))[:, None], (8, 128))
        mem, seg = run_window(
            segments[rnd:rnd + 1], memory, lengths, norm_gain, w_query, w_key, value_weight, w_out)
        mem_states.append(mem)
        seg_states.append(seg)
        if rnd + 1 < rounds:
            shared = lax.ppermute(mem[0, 0], "phase", [(1, 0), (0, 1)])
            memory = route_memory(shared, routes)
    return jnp.concatenate(mem_states, axis=1), jnp.concatenate(seg_states, axis=1)


def solution(mesh):
    return jax.shard_map(
        per_device,
        mesh=mesh,
        in_specs=(
            P(None, "dp", "mp", None),
            P("dp", "mp", None),
            P(None, "dp"),
            P(),
            P("phase", None, "mp"),
            P("phase", None, "mp"),
            P("phase", None, "mp"),
            P("phase", "mp", None),
            P("phase", None),
        ),
        out_specs=(P("phase", None, "dp", "mp", None), P("phase", None, "dp", "mp", None)),
        check_vma=False,
    )
```

```python
import functools

import jax
import jax.numpy as jnp
from jax import lax
from jax.experimental import pallas as pl
from jax.experimental.pallas import tpu as pltpu
from jax.sharding import PartitionSpec as P

HEAD_SIZE = 128
EPSILON = 1e-05
CHUNKS = 4
TILE = 1024
PIECE = 128
MESH = pl.DeviceIdType.MESH


def window_kernel(
    segments, memory, lengths, origins, gain, w_query, w_key, w_value, w_out,
    mem_out, seg_out,
    wq, wk, wv, wo, gathered, rows_home, partial, received, normed, queries, keys, values, attended, far_lengths, spread_even, spread_odd, picked,
    wq_sem, wk_sem, wv_sem, wo_sem, len_sem, gather_send, gather_recv, home_send, home_recv, sum_send, sum_recv, out_sem,
    route_send, route_recv, back_send, back_recv,
):
    phase = lax.axis_index("phase")
    group = lax.axis_index("dp")
    half = lax.axis_index("mp")
    groups = lax.axis_size("dp")
    spread = (spread_even, spread_odd)
    across = group + 1 - 2 * (group % 2)
    rounds, slots, dev_rows, width = segments.shape
    block = 2 * dev_rows
    items = rounds * slots
    chunk = width // CHUNKS
    first = phase == 0
    second = phase == 1

    def weight_copies():
        copies = []
        for tile in range(wq.shape[1] // TILE):
            cols = pl.ds(tile * TILE, TILE)
            copies.append(pltpu.make_async_copy(w_query.at[0, :, cols], wq.at[:, cols], wq_sem.at[tile]))
        copies.append(pltpu.make_async_copy(w_key.at[0], wk, wk_sem))
        copies.append(pltpu.make_async_copy(w_value.at[0], wv, wv_sem))
        for tile in range(wo.shape[1] // TILE):
            cols = pl.ds(tile * TILE, TILE)
            copies.append(pltpu.make_async_copy(w_out.at[0, :, cols], wo.at[:, cols], wo_sem.at[tile]))
        return copies

    def length_copy():
        return pltpu.make_async_remote_copy(
            src_ref=lengths, dst_ref=far_lengths, send_sem=len_sem.at[0], recv_sem=len_sem.at[1],
            device_id=(phase, across, half), device_id_type=MESH,
        )

    def row_copies(item, source, kind):
        return [
            pltpu.make_async_remote_copy(
                src_ref=source,
                dst_ref=gathered.at[item, pl.ds(pl.multiple_of(half * block + kind * dev_rows, dev_rows), dev_rows)],
                send_sem=gather_send.at[item, target, kind],
                recv_sem=gather_recv.at[item, half, kind],
                device_id=(0, across, target), device_id_type=MESH,
            )
            for target in range(2)
        ]

    def memory_copies(item):
        return row_copies(item, memory.at[item], 0)

    def segment_copies(item):
        return row_copies(item, segments.at[item // slots, item % slots], 1)

    def routed_copies(item):
        return row_copies(item, rows_home.at[item, pl.ds(0, dev_rows)], 0)

    def own_memory(item):
        return pltpu.make_async_copy(memory.at[item], rows_home.at[item, pl.ds(0, dev_rows)], home_recv.at[item, 0])

    def own_segment(item):
        return pltpu.make_async_copy(
            segments.at[item // slots, item % slots], rows_home.at[item, pl.ds(dev_rows, dev_rows)], home_recv.at[item, 1])

    def piece_copy(slot, piece):
        return pltpu.make_async_remote_copy(
            src_ref=rows_home.at[slot, pl.ds(0, dev_rows), pl.ds(pl.multiple_of(piece * PIECE, PIECE), PIECE)],
            dst_ref=spread[slot].at[group],
            send_sem=route_send.at[slot], recv_sem=route_recv.at[slot],
            device_id=(0, piece, half), device_id_type=MESH,
        )

    own_piece = pl.ds(pl.multiple_of(group * PIECE, PIECE), PIECE)

    def middle(slot):
        pltpu.make_async_copy(spread[slot], spread[slot], route_recv.at[slot]).wait()
        item = slots + slot
        rows_home[item, pl.ds(0, dev_rows), own_piece] = spread[slot][origins[slot, group]]

        @pl.loop(1, groups)
        def _(step):
            target = (group + step) % groups
            picked[slot, target] = spread[slot][origins[slot, target]]
            pltpu.make_async_remote_copy(
                src_ref=picked.at[slot, target],
                dst_ref=rows_home.at[item, pl.ds(0, dev_rows), own_piece],
                send_sem=back_send.at[slot], recv_sem=back_recv.at[slot],
                device_id=(0, target, half), device_id_type=MESH,
            ).start()

    def forward(slot):
        item = slots + slot
        here = picked.at[slot, pl.ds(0, groups - 1)]
        pltpu.make_async_copy(here, here, back_recv.at[slot]).wait()
        for copy in routed_copies(item):
            copy.start()

    def hand_copies(item, index):
        cols = pl.ds(pl.multiple_of(index * chunk, chunk), chunk)
        far = []
        for target in range(2):
            far.append(pltpu.make_async_remote_copy(
                src_ref=rows_home.at[item, :, cols],
                dst_ref=gathered.at[item, pl.ds(pl.multiple_of(half * block, block), block), cols],
                send_sem=gather_send.at[item, target, index],
                recv_sem=gather_recv.at[item, half, index],
                device_id=(1, across, target), device_id_type=MESH,
            ))
        far.append(pltpu.make_async_remote_copy(
            src_ref=rows_home.at[item, :, cols], dst_ref=rows_home.at[item, :, cols],
            send_sem=home_send.at[item, index], recv_sem=home_recv.at[item, index],
            device_id=(1, group, half), device_id_type=MESH,
        ))
        return far

    def sum_copy(item, index, target):
        cols = pl.ds(pl.multiple_of(index * chunk, chunk), chunk)
        return pltpu.make_async_remote_copy(
            src_ref=partial.at[item, pl.ds(target * block, block), cols],
            dst_ref=received.at[item, half, :, cols],
            send_sem=sum_send.at[item, index, target],
            recv_sem=sum_recv.at[item, half, index],
            device_id=(phase, across, target), device_id_type=MESH,
        )

    def out_copies(item):
        rnd, slot = item // slots, item % slots
        return (
            pltpu.make_async_copy(rows_home.at[item, pl.ds(0, dev_rows)], mem_out.at[0, rnd, slot], out_sem.at[item, 0]),
            pltpu.make_async_copy(rows_home.at[item, pl.ds(dev_rows, dev_rows)], seg_out.at[0, rnd, slot], out_sem.at[item, 1]),
        )

    barrier = pltpu.get_barrier_semaphore()
    for target in range(2):
        pl.semaphore_signal(barrier, inc=1, device_id=(phase, across, target), device_id_type=MESH)

    @pl.when(second)
    def _():
        for target in range(2):
            pl.semaphore_signal(barrier, inc=1, device_id=(0, across, target), device_id_type=MESH)
        pl.semaphore_signal(barrier, inc=1, device_id=(0, group, half), device_id_type=MESH)

    for copy in weight_copies():
        copy.start()

    @pl.when(first)
    def _():
        @pl.loop(0, groups)
        def _(target):
            pl.semaphore_signal(barrier, inc=1, device_id=(1, target, half), device_id_type=MESH)

        @pl.loop(1, groups)
        def _(step):
            pl.semaphore_signal(barrier, inc=1, device_id=(0, (group + step) % groups, half), device_id_type=MESH)

        pl.semaphore_wait(barrier, 5 + groups - 1)

    @pl.when(second)
    def _():
        pl.semaphore_wait(barrier, 2 + groups)

    length_copy().start()

    @pl.when(first)
    def _():
        @pl.loop(0, slots)
        def _(item):
            for copy in memory_copies(item) + segment_copies(item):
                copy.start()
            own_memory(item).start()

        @pl.loop(0, items)
        def _(item):
            own_segment(item).start()

    length_copy().wait()

    def positions(axis):
        index = lax.broadcasted_iota(jnp.int32, (2 * block, 2 * block), axis)
        part, within = index // block, index % block
        return jnp.where(within < dev_rows, part * dev_rows + within, block + part * dev_rows + within - dev_rows)

    def project(item):
        @pl.when(first)
        def _():
            for origin in range(2):
                for kind in range(2):
                    here = gathered.at[item, pl.ds(origin * block + kind * dev_rows, dev_rows)]
                    pltpu.make_async_copy(here, here, gather_recv.at[item, origin, kind]).wait()

        @pl.when(second)
        def _():
            for origin in range(2):
                for index in range(CHUNKS):
                    here = gathered.at[item, pl.ds(origin * block, block), pl.ds(index * chunk, chunk)]
                    pltpu.make_async_copy(here, here, gather_recv.at[item, origin, index]).wait()

        scale_row = gain[...].astype(jnp.float32)

        @pl.loop(0, 2 * block // 16)
        def _(step):
            rows = pl.ds(pl.multiple_of(step * 16, 16), 16)
            x = gathered[item, rows].astype(jnp.float32)
            scaled = x * lax.rsqrt(jnp.mean(x * x, axis=-1, keepdims=True) + EPSILON)
            normed[rows] = (scaled * scale_row).astype(jnp.bfloat16)

        @pl.loop(0, wq.shape[1] // TILE)
        def _(tile):
            cols = pl.ds(pl.multiple_of(tile * TILE, TILE), TILE)

            @pl.when(item == 0)
            def _():
                pltpu.make_async_copy(w_query.at[0, :, cols], wq.at[:, cols], wq_sem.at[tile]).wait()

            queries[:, cols] = jnp.dot(normed[...], wq[:, cols], preferred_element_type=jnp.float32).astype(jnp.bfloat16)

    def attend(item):
        @pl.when(item == 0)
        def _():
            pltpu.make_async_copy(w_key.at[0], wk, wk_sem).wait()
            pltpu.make_async_copy(w_value.at[0], wv, wv_sem).wait()

        keys[...] = jnp.dot(normed[...], wk[...], preferred_element_type=jnp.float32).astype(jnp.bfloat16)
        values[...] = jnp.dot(normed[...], wv[...], preferred_element_type=jnp.float32).astype(jnp.bfloat16)

        length = far_lengths[pl.ds(item, 1), :]
        query_pos, key_pos = positions(0), positions(1)
        visible = (key_pos < block) | (key_pos - block < length) & ((query_pos < block) | (key_pos <= query_pos))
        heads = wq.shape[1] // HEAD_SIZE
        kv_heads = wk.shape[1] // HEAD_SIZE
        per = heads // kv_heads
        seen = jnp.concatenate([visible] * per, axis=0)
        for kv in range(kv_heads):
            k = keys[:, kv * HEAD_SIZE:(kv + 1) * HEAD_SIZE]
            v = values[:, kv * HEAD_SIZE:(kv + 1) * HEAD_SIZE]
            q = jnp.concatenate(
                [queries[:, head * HEAD_SIZE:(head + 1) * HEAD_SIZE] for head in range(kv * per, (kv + 1) * per)], axis=0)
            scores = lax.dot_general(q, k, (((1,), (1,)), ((), ())), preferred_element_type=jnp.float32)
            scores = jnp.where(seen, scores * HEAD_SIZE ** (-0.5), -1e30)
            weights = jnp.exp(scores - jnp.max(scores, axis=-1, keepdims=True))
            attn = (weights * (1.0 / jnp.sum(weights, axis=-1, keepdims=True))).astype(jnp.bfloat16)
            mixed = jnp.dot(attn, v, preferred_element_type=jnp.float32).astype(jnp.bfloat16)
            for step in range(per):
                head = kv * per + step
                attended[:, head * HEAD_SIZE:(head + 1) * HEAD_SIZE] = mixed[step * 2 * block:(step + 1) * 2 * block]

        @pl.loop(0, CHUNKS)
        def _(index):
            for step in range(chunk // TILE):
                tile = index * (chunk // TILE) + step
                cols = pl.ds(pl.multiple_of(tile * TILE, TILE), TILE)

                @pl.when(item == 0)
                def _():
                    pltpu.make_async_copy(w_out.at[0, :, cols], wo.at[:, cols], wo_sem.at[tile]).wait()

                partial[item, :, cols] = jnp.dot(
                    attended[...], wo[:, cols], preferred_element_type=jnp.float32).astype(jnp.bfloat16)
            for target in range(2):
                sum_copy(item, index, target).start()

    def home(item, slot):
        @pl.when(first)
        def _():
            own_segment(item).wait()

            @pl.when(item < slots)
            def _():
                own_memory(slot).wait()

            @pl.when(item >= slots)
            def _():
                for copy in routed_copies(item):
                    copy.wait_send()

        @pl.loop(0, CHUNKS)
        def _(index):
            cols = pl.ds(pl.multiple_of(index * chunk, chunk), chunk)

            @pl.when(second)
            def _():
                here = rows_home.at[item, :, cols]
                pltpu.make_async_copy(here, here, home_recv.at[item, index]).wait()

            for origin in range(2):
                here = received.at[item, origin, :, cols]
                pltpu.make_async_copy(here, here, sum_recv.at[item, origin, index]).wait()
            total = received[item, 0, :, cols].astype(jnp.float32) + received[item, 1, :, cols].astype(jnp.float32)
            rows_home[item, :, cols] = (rows_home[item, :, cols].astype(jnp.float32) + total).astype(jnp.bfloat16)

            @pl.when(first)
            def _():
                for copy in hand_copies(item, index):
                    copy.start()

            @pl.when(second & (item < slots))
            def _():
                @pl.loop(0, groups // CHUNKS)
                def _(step):
                    piece_copy(slot, index * (groups // CHUNKS) + step).start()

        for copy in out_copies(item):
            copy.start()

    @pl.loop(0, items)
    def _(item):
        later = first & (item == slots)

        @pl.when(later)
        def _():
            middle(0)
            forward(0)

        project(item)

        @pl.when(item % 2 == 1)
        def _():
            home(item - 1, 0)

        @pl.when(first & (item == 0))
        def _():
            @pl.loop(slots, items)
            def _(other):
                for copy in segment_copies(other):
                    copy.start()

        @pl.when(later)
        def _():
            middle(1)

        attend(item)

        @pl.when(later)
        def _():
            forward(1)

        @pl.when(item % 2 == 1)
        def _():
            home(item, 1)

    @pl.loop(0, items)
    def _(item):
        for copy in out_copies(item):
            copy.wait()

        @pl.loop(0, CHUNKS)
        def _(index):
            for target in range(2):
                sum_copy(item, index, target).wait_send()

        @pl.when(first)
        def _():
            for copy in segment_copies(item):
                copy.wait_send()

            @pl.loop(0, CHUNKS)
            def _(index):
                for copy in hand_copies(item, index):
                    copy.wait_send()

    for slot in range(slots):
        @pl.when(first)
        def _():
            for copy in memory_copies(slot):
                copy.wait_send()
            here = picked.at[slot, pl.ds(0, groups - 1)]
            pltpu.make_async_copy(here, here, back_send.at[slot]).wait()

        @pl.when(second)
        def _():
            pltpu.make_async_copy(spread[slot], spread[slot], route_send.at[slot]).wait()


def run_window(segments, memory, lengths, origins, gain, w_query, w_key, w_value, w_out):
    rounds, slots, dev_rows, width = segments.shape
    items = rounds * slots
    block = 2 * dev_rows
    rows = 2 * block
    bf16 = jnp.bfloat16
    dma = pltpu.SemaphoreType.DMA
    states = jax.ShapeDtypeStruct((1, rounds, slots, dev_rows, width), bf16)
    return pl.pallas_call(
        window_kernel,
        out_shape=(states, states),
        in_specs=[pl.BlockSpec(memory_space=pl.ANY)] * 2
        + [pl.BlockSpec(memory_space=pltpu.VMEM), pl.BlockSpec(memory_space=pltpu.SMEM), pl.BlockSpec(memory_space=pltpu.VMEM)]
        + [pl.BlockSpec(memory_space=pl.ANY)] * 4,
        out_specs=(pl.BlockSpec(memory_space=pl.ANY), pl.BlockSpec(memory_space=pl.ANY)),
        scratch_shapes=[
            pltpu.VMEM(w_query.shape[1:], bf16),
            pltpu.VMEM(w_key.shape[1:], bf16),
            pltpu.VMEM(w_value.shape[1:], bf16),
            pltpu.VMEM(w_out.shape[1:], bf16),
            pltpu.VMEM((items, rows, width), bf16),
            pltpu.VMEM((items, block, width), bf16),
            pltpu.VMEM((items, rows, width), bf16),
            pltpu.VMEM((items, 2, block, width), bf16),
            pltpu.VMEM((rows, width), bf16),
            pltpu.VMEM((rows, w_query.shape[2]), bf16),
            pltpu.VMEM((rows, w_key.shape[2]), bf16),
            pltpu.VMEM((rows, w_value.shape[2]), bf16),
            pltpu.VMEM((rows, w_query.shape[2]), bf16),
            pltpu.VMEM(lengths.shape, jnp.int32),
            pltpu.VMEM((width // PIECE, dev_rows, PIECE), bf16),
            pltpu.VMEM((width // PIECE, dev_rows, PIECE), bf16),
            pltpu.VMEM((slots, width // PIECE, dev_rows, PIECE), bf16),
            dma((w_query.shape[2] // TILE,)),
            dma,
            dma,
            dma((width // TILE,)),
            dma((2,)),
            dma((items, 2, CHUNKS)),
            dma((items, 2, CHUNKS)),
            dma((items, CHUNKS)),
            dma((items, CHUNKS)),
            dma((items, CHUNKS, 2)),
            dma((items, 2, CHUNKS)),
            dma((items, 2)),
            dma((slots,)),
            dma((slots,)),
            dma((slots,)),
            dma((slots,)),
        ],
        compiler_params=pltpu.CompilerParams(
            collective_id=0, has_side_effects=True, vmem_limit_bytes=62 * 1024 * 1024
        ),
    )(segments, memory, lengths, origins, gain, w_query, w_key, w_value, w_out)


def per_device(segments, memory_in, seg_lengths, routes, w_query, w_key, value_weight, w_out, norm_gain):
    groups = routes.shape[1]
    lengths = jnp.broadcast_to(jnp.pad(seg_lengths.reshape(-1), (0, 8 - seg_lengths.size))[:, None], (8, 128))
    ids = jnp.arange(groups, dtype=jnp.int32)
    origins = jnp.sum(jnp.where(routes[:, None, :] == ids[None, :, None], ids[None, None, :], 0), axis=-1)
    return run_window(
        segments, memory_in, lengths, origins, norm_gain, w_query, w_key, value_weight, w_out)


def solution(mesh):
    return jax.shard_map(
        per_device,
        mesh=mesh,
        in_specs=(
            P(None, "dp", "mp", None),
            P("dp", "mp", None),
            P(None, "dp"),
            P(),
            P("phase", None, "mp"),
            P("phase", None, "mp"),
            P("phase", None, "mp"),
            P("phase", "mp", None),
            P("phase", None),
        ),
        out_specs=(P("phase", None, "dp", "mp", None), P("phase", None, "dp", "mp", None)),
        check_vma=False,
    )
```

```python
import jax
import jax.numpy as jnp
from jax import lax
from jax.experimental import pallas as pl
from jax.experimental.pallas import tpu as pltpu
from jax.sharding import PartitionSpec as P

HEAD_SIZE = 128
EPSILON = 1e-05
CHUNKS = 4
AHEAD = 4
PIECE = 128
BAND = 32
MESH = pl.DeviceIdType.MESH
F32 = jnp.float32
BF16 = jnp.bfloat16


def window_kernel(
    segments, memory, lengths, routes, gain, w_query, w_key, w_value, w_out,
    mem_out, seg_out,
    wq, wk, wv, wo, rows_in, partial, own_sum, far_sum, last_sum, scaled, squares, acc_q, acc_k, acc_v,
    queries, keys, values, attended, spread_even, spread_odd, picked, origins,
    win_sem, wo_sem, own_sem, gather_send, gather_recv, keep_send, keep_recv, far_send, far_recv, near_send, near_recv,
    mem_send, mem_recv, seg_send, seg_recv, state_send, state_recv, out_sem, route_send, route_recv, back_send, back_recv, known_sem,
):
    phase = lax.axis_index("phase")
    group = lax.axis_index("dp")
    half = lax.axis_index("mp")
    groups = lax.axis_size("dp")
    peer = 1 - half
    rounds, slots, dev_rows, width = segments.shape
    mem_rows = 2 * dev_rows
    rows = 2 * mem_rows
    items = rounds * slots
    chunk = width // CHUNKS
    first = phase == 0
    second = phase == 1
    spread = (spread_even, spread_odd)
    mem_home = pl.multiple_of(half * dev_rows, dev_rows)
    seg_home = pl.multiple_of(mem_rows + half * dev_rows, dev_rows)
    mem_peer = pl.multiple_of(peer * dev_rows, dev_rows)
    seg_peer = pl.multiple_of(mem_rows + peer * dev_rows, dev_rows)

    def columns(index):
        return pl.ds(pl.multiple_of(index * chunk, chunk), chunk)

    def arrived(ref, sem):
        pltpu.make_async_copy(ref, ref, sem).wait()

    def remote(source, target, send, recv, device):
        return pltpu.make_async_remote_copy(
            src_ref=source, dst_ref=target, send_sem=send, recv_sem=recv, device_id=device, device_id_type=MESH)

    def in_copies(index):
        depth = pl.ds(index * chunk, chunk)
        return [
            pltpu.make_async_copy(source.at[0, depth], target.at[depth], win_sem.at[index, which])
            for which, (source, target) in enumerate(((w_query, wq), (w_key, wk), (w_value, wv)))
        ]

    def wo_copy(index):
        cols = columns(index)
        return pltpu.make_async_copy(w_out.at[0, :, cols], wo.at[:, cols], wo_sem.at[index])

    def entry_source(item, kind):
        return memory.at[item] if kind == 0 else segments.at[item // slots, item % slots]

    def entry_own(item, kind):
        return pltpu.make_async_copy(
            entry_source(item, kind), rows_in.at[item, pl.ds((mem_home, seg_home)[kind], dev_rows)], own_sem.at[item, kind])

    def entry_far(item, kind, index):
        cols = pl.ds(index * chunk, chunk)
        return remote(entry_source(item, kind).at[:, cols],
                      rows_in.at[item, pl.ds((mem_home, seg_home)[kind], dev_rows), cols],
                      gather_send.at[item, kind, index], gather_recv.at[item, kind, index], (0, group, peer))

    def entry_wait(item, kind, index):
        cols = pl.ds(index * chunk, chunk)
        arrived(rows_in.at[item, pl.ds((mem_peer, seg_peer)[kind], dev_rows), cols], gather_recv.at[item, kind, index])

    def keep_copy(item):
        return remote(rows_in.at[item], rows_in.at[item], keep_send.at[item], keep_recv.at[item], (1, group, half))

    def far_copy(item, index):
        slot, cols = item % slots, columns(index)
        return remote(partial.at[slot, :, cols], far_sum.at[slot, :, cols], far_send.at[item, index],
                      far_recv.at[item, index], (1, group, peer))

    def near_copy(item, index):
        slot, cols = item % slots, columns(index)
        return remote(partial.at[slot, :, cols], own_sum.at[slot, :, cols], near_send.at[item, index],
                      near_recv.at[item, index], (1, group, half))

    def mem_all(item, index):
        slot, cols = item % slots, columns(index)
        span = pl.ds(0, mem_rows)
        return remote(partial.at[slot, span, cols], last_sum.at[item, span, cols], mem_send.at[item, index],
                      mem_recv.at[item, index], (1, group, peer))

    def mem_part(item, index):
        slot, cols = item % slots, columns(index)
        return remote(partial.at[slot, pl.ds(mem_peer, dev_rows), cols], last_sum.at[item, pl.ds(0, dev_rows), cols],
                      mem_send.at[item, index], mem_recv.at[item, index], (1, group, peer))

    def seg_part(item):
        slot = item % slots
        return remote(partial.at[slot, pl.ds(seg_peer, dev_rows)], last_sum.at[item, pl.ds(mem_rows, dev_rows)],
                      seg_send.at[item], seg_recv.at[item], (1, group, peer))

    def states(item):
        rnd, slot = item // slots, item % slots
        return ((rows_in.at[item, pl.ds(mem_home, dev_rows)], mem_out.at[0, rnd, slot]),
                (rows_in.at[item, pl.ds(seg_home, dev_rows)], seg_out.at[0, rnd, slot]))

    def state_copies(item):
        return [remote(source, target, state_send.at[item, kind], state_recv.at[item, kind], (0, group, half))
                for kind, (source, target) in enumerate(states(item))]

    def out_copy(item, kind):
        source, target = states(item)[kind]
        return pltpu.make_async_copy(source, target, out_sem.at[item, kind])

    own_piece = pl.ds(pl.multiple_of(group * PIECE, PIECE), PIECE)

    def piece_copy(slot, piece):
        return remote(rows_in.at[slot, pl.ds(0, mem_rows), pl.ds(pl.multiple_of(piece * PIECE, PIECE), PIECE)],
                      spread[slot].at[group], route_send.at[slot], route_recv.at[slot], (0, piece, half))

    def reorder(slot):
        item = slots + slot
        arrived(spread[slot], route_recv.at[slot])
        for index in range(CHUNKS):
            entry_far(item, 1, index).start()
        rows_in[item, pl.ds(0, mem_rows), own_piece] = spread[slot][origins[slot, group]]

        @pl.loop(1, groups)
        def _(step):
            target = (group + step) % groups
            picked[slot, target] = spread[slot][origins[slot, target]]
            remote(picked.at[slot, target], rows_in.at[item, pl.ds(0, mem_rows), own_piece],
                   back_send.at[slot], back_recv.at[slot], (0, target, half)).start()

        arrived(picked.at[slot, pl.ds(0, groups - 1)], back_recv.at[slot])

    barrier = pltpu.get_barrier_semaphore()

    def greet(device):
        pl.semaphore_signal(barrier, inc=1, device_id=device, device_id_type=MESH)

    greet((phase, group, peer))

    @pl.when(second)
    def _():
        greet((0, group, half))
        greet((0, group, peer))

    for index in range(AHEAD):
        for copy in in_copies(index):
            copy.start()

    plane, line, side = group // 8, group // 2 % 4, group % 2
    line_mates = [(0, group + ((line + step) % 4 - line) * 2, half) for step in range(1, 4)]
    plane_mates = [(0, group + ((plane + step) % 4 - plane) * 8, half) for step in range(1, 4)]
    side_mate = (0, group + 1 - 2 * side, half)

    def tell(index, device):
        pl.semaphore_signal(known_sem.at[index], inc=1, device_id=device, device_id_type=MESH)

    @pl.when(first)
    def _():
        for device in line_mates + plane_mates + [side_mate, (1, group, half)]:
            greet(device)
        pl.semaphore_wait(barrier, 10)

        for item in range(slots):
            for kind in range(2):
                entry_own(item, kind).start()
            for index in range(CHUNKS):
                for kind in range(2):
                    entry_far(item, kind, index).start()
        for item in range(slots, items):
            entry_own(item, 1).start()
        for device in plane_mates:
            tell(0, device)

        for slot in range(slots):
            @pl.loop(0, groups)
            def _(target):
                origin = jnp.int32(0)
                for source in range(groups):
                    origin = jnp.where(routes[slot, source] == target, source, origin)
                origins[slot, target] = origin

        pl.semaphore_wait(known_sem.at[0], 3)
        tell(1, side_mate)

    @pl.when(second)
    def _():
        pl.semaphore_wait(barrier, 2)

    def project(item):
        slot = item % slots

        @pl.when(first)
        def _():
            @pl.when(item < slots)
            def _():
                entry_own(slot, 0).wait()
            entry_own(item, 1).wait()

        for index in range(CHUNKS):
            cols = pl.ds(index * chunk, chunk)

            @pl.when(first)
            def _():
                @pl.when(item < slots)
                def _():
                    entry_wait(slot, 0, index)
                entry_wait(item, 1, index)

            @pl.when(second)
            def _():
                if index == 0:
                    arrived(rows_in.at[item], keep_recv.at[item])
                arrived(own_sum.at[slot, :, cols], near_recv.at[item, index])
                arrived(far_sum.at[slot, :, cols], far_recv.at[item, index])

                @pl.loop(0, rows // BAND)
                def _(band):
                    span = pl.ds(pl.multiple_of(band * BAND, BAND), BAND)
                    total = own_sum[slot, span, cols].astype(F32) + far_sum[slot, span, cols].astype(F32)
                    rows_in[item, span, cols] = (rows_in[item, span, cols].astype(F32) + total).astype(BF16)

            gain_row = gain[:, cols].astype(F32)

            @pl.loop(0, rows // BAND)
            def _(band):
                span = pl.ds(pl.multiple_of(band * BAND, BAND), BAND)
                x = rows_in[item, span, cols].astype(F32)
                scaled[span] = (x * gain_row).astype(BF16)
                square = x * x
                lanes = square[:, :128]
                for step in range(1, chunk // 128):
                    lanes = lanes + square[:, step * 128:(step + 1) * 128]
                squares[span] = lanes if index == 0 else squares[span] + lanes

            @pl.when(item == 0)
            def _():
                for copy in in_copies(index):
                    copy.wait()
                if index + AHEAD < CHUNKS:
                    for copy in in_copies(index + AHEAD):
                        copy.start()
                else:
                    for other in range(CHUNKS // AHEAD):
                        wo_copy((index + AHEAD - CHUNKS) * (CHUNKS // AHEAD) + other).start()

            depth = pl.ds(index * chunk, chunk)
            for weights, acc in ((wq, acc_q), (wk, acc_k), (wv, acc_v)):
                for start in range(0, weights.shape[1], 512):
                    part = pl.ds(start, 512)
                    product = jnp.dot(scaled[...], weights[depth, part], preferred_element_type=F32)
                    acc[:, part] = product if index == 0 else acc[:, part] + product

        @pl.when(first)
        def _():
            keep_copy(item).start()

        @pl.when(second)
        def _():
            for copy in state_copies(item):
                copy.start()

        @pl.loop(0, rows // BAND)
        def _(band):
            span = pl.ds(pl.multiple_of(band * BAND, BAND), BAND)
            factor = lax.rsqrt(jnp.sum(squares[span], axis=-1, keepdims=True) * (1.0 / width) + EPSILON)
            queries[span] = (acc_q[span] * factor).astype(BF16)
            keys[span] = (acc_k[span] * factor).astype(BF16)
            values[span] = (acc_v[span] * factor).astype(BF16)

    def attend(item):
        length = lengths[item // slots, item % slots]
        query_pos = lax.broadcasted_iota(jnp.int32, (rows, rows), 0)
        key_pos = lax.broadcasted_iota(jnp.int32, (rows, rows), 1)
        visible = (key_pos < mem_rows) | (key_pos - mem_rows < length) & (
            (query_pos < mem_rows) | (key_pos <= query_pos))
        heads = wq.shape[1] // HEAD_SIZE
        kv_heads = wk.shape[1] // HEAD_SIZE
        per = heads // kv_heads
        seen = jnp.concatenate([visible] * per, axis=0)
        for kv in range(kv_heads):
            k = keys[:, kv * HEAD_SIZE:(kv + 1) * HEAD_SIZE]
            v = values[:, kv * HEAD_SIZE:(kv + 1) * HEAD_SIZE]
            q = jnp.concatenate(
                [queries[:, head * HEAD_SIZE:(head + 1) * HEAD_SIZE] for head in range(kv * per, (kv + 1) * per)], axis=0)
            scores = lax.dot_general(q, k, (((1,), (1,)), ((), ())), preferred_element_type=F32)
            scores = jnp.where(seen, scores * HEAD_SIZE ** (-0.5), -1e30)
            weights = jnp.exp(scores - jnp.max(scores, axis=-1, keepdims=True))
            attn = (weights * (1.0 / jnp.sum(weights, axis=-1, keepdims=True))).astype(BF16)
            mixed = jnp.dot(attn, v, preferred_element_type=F32).astype(BF16)
            for step in range(per):
                head = kv * per + step
                attended[:, head * HEAD_SIZE:(head + 1) * HEAD_SIZE] = mixed[step * rows:(step + 1) * rows]

    def emit(item):
        slot = item % slots
        last = item >= items - slots

        @pl.when(item >= slots)
        def _():
            before = item - slots

            @pl.when(first)
            def _():
                for index in range(CHUNKS):
                    far_copy(before, index).wait_send()
                    near_copy(before, index).wait_send()

            @pl.when(second)
            def _():
                for index in range(CHUNKS):
                    mem_all(before, index).wait_send()
                seg_part(before).wait_send()

        for index in range(CHUNKS):
            cols = pl.ds(index * chunk, chunk)

            @pl.when(item == 0)
            def _():
                wo_copy(index).wait()

            partial[slot, :, cols] = jnp.dot(attended[...], wo[:, cols], preferred_element_type=F32).astype(BF16)

            @pl.when(first)
            def _():
                far_copy(item, index).start()
                near_copy(item, index).start()

            @pl.when(second & jnp.logical_not(last))
            def _():
                mem_all(item, index).start()

            @pl.when(second & last)
            def _():
                mem_part(item, index).start()

        @pl.when(second)
        def _():
            seg_part(item).start()

    def add_rows(item, cols, start, landed, count):
        slot = item % slots

        @pl.loop(0, count // BAND)
        def _(band):
            span = pl.ds(pl.multiple_of(start + band * BAND, BAND), BAND)
            there = pl.ds(pl.multiple_of(landed + band * BAND, BAND), BAND)
            total = partial[slot, span, cols].astype(F32) + last_sum[item, there, cols].astype(F32)
            rows_in[item, span, cols] = (rows_in[item, span, cols].astype(F32) + total).astype(BF16)

    def finish_memory(item, slot):
        state = state_copies(item)
        for copy in state:
            copy.wait_send()

        @pl.when(item < items - slots)
        def _():
            if slot == 0:
                pl.semaphore_wait(known_sem.at[2], 1)

            @pl.loop(0, CHUNKS)
            def _(index):
                cols = columns(index)
                arrived(last_sum.at[item, pl.ds(0, mem_rows), cols], mem_recv.at[item, index])
                add_rows(item, cols, 0, 0, mem_rows)

                @pl.loop(0, groups // CHUNKS)
                def _(step):
                    piece_copy(slot, index * (groups // CHUNKS) + step).start()

        @pl.when(item >= items - slots)
        def _():
            @pl.loop(0, CHUNKS)
            def _(index):
                cols = columns(index)
                arrived(last_sum.at[item, pl.ds(0, dev_rows), cols], mem_recv.at[item, index])
                add_rows(item, cols, mem_home, 0, dev_rows)

        out_copy(item, 0).start()

    def finish_segment(item):
        arrived(last_sum.at[item, pl.ds(mem_rows, dev_rows)], seg_recv.at[item])

        @pl.loop(0, CHUNKS)
        def _(index):
            add_rows(item, columns(index), seg_home, mem_rows, dev_rows)

        out_copy(item, 1).start()

    @pl.loop(0, items)
    def _(item):
        @pl.when(first & (item == slots))
        def _():
            reorder(0)

        @pl.when(first & (item == slots + 1))
        def _():
            reorder(1)

        project(item)

        @pl.when(first & (item == 0))
        def _():
            pl.semaphore_wait(known_sem.at[1], 1)
            tell(2, (1, group, half))

        @pl.when(second & (item % slots == 1))
        def _():
            finish_memory(item - 1, 0)

        attend(item)
        emit(item)

        @pl.when(second & (item % slots == 1))
        def _():
            finish_memory(item, 1)
            finish_segment(item - 1)
            finish_segment(item)

    @pl.loop(0, items)
    def _(item):
        last = item >= items - slots

        @pl.when(first)
        def _():
            for source, target in states(item)[:1]:
                arrived(target, state_recv.at[item, 0])
            for source, target in states(item)[1:]:
                arrived(target, state_recv.at[item, 1])
            for index in range(CHUNKS):
                entry_far(item, 1, index).wait_send()
            keep_copy(item).wait_send()

            @pl.when(last)
            def _():
                for index in range(CHUNKS):
                    far_copy(item, index).wait_send()
                    near_copy(item, index).wait_send()

        @pl.when(second)
        def _():
            out_copy(item, 0).wait()
            out_copy(item, 1).wait()

            @pl.when(last)
            def _():
                for index in range(CHUNKS):
                    mem_part(item, index).wait_send()
                seg_part(item).wait_send()

    for slot in range(slots):
        @pl.when(first)
        def _():
            for index in range(CHUNKS):
                entry_far(slot, 0, index).wait_send()
            arrived(picked.at[slot, pl.ds(0, groups - 1)], back_send.at[slot])

        @pl.when(second)
        def _():
            arrived(spread[slot], route_send.at[slot])


def run_window(segments, memory, lengths, routes, gain, w_query, w_key, w_value, w_out):
    rounds, slots, dev_rows, width = segments.shape
    items = rounds * slots
    mem_rows = 2 * dev_rows
    rows = 2 * mem_rows
    groups = width // PIECE
    dma = pltpu.SemaphoreType.DMA
    vmem = pltpu.VMEM
    states = jax.ShapeDtypeStruct((1, rounds, slots, dev_rows, width), BF16)
    q_width, kv_width = w_query.shape[2], w_key.shape[2]
    return pl.pallas_call(
        window_kernel,
        out_shape=(states, states),
        in_specs=[pl.BlockSpec(memory_space=pl.ANY)] * 2
        + [pl.BlockSpec(memory_space=pltpu.SMEM)] * 2
        + [pl.BlockSpec(memory_space=vmem)]
        + [pl.BlockSpec(memory_space=pl.ANY)] * 4,
        out_specs=(pl.BlockSpec(memory_space=pl.ANY), pl.BlockSpec(memory_space=pl.ANY)),
        scratch_shapes=[
            vmem(w_query.shape[1:], BF16),
            vmem(w_key.shape[1:], BF16),
            vmem(w_value.shape[1:], BF16),
            vmem(w_out.shape[1:], BF16),
            vmem((items, rows, width), BF16),
            vmem((slots, rows, width), BF16),
            vmem((slots, rows, width), BF16),
            vmem((slots, rows, width), BF16),
            vmem((items, mem_rows + dev_rows, width), BF16),
            vmem((rows, width // CHUNKS), BF16),
            vmem((rows, 128), F32),
            vmem((rows, q_width), F32),
            vmem((rows, kv_width), F32),
            vmem((rows, kv_width), F32),
            vmem((rows, q_width), BF16),
            vmem((rows, kv_width), BF16),
            vmem((rows, kv_width), BF16),
            vmem((rows, q_width), BF16),
            vmem((groups, mem_rows, PIECE), BF16),
            vmem((groups, mem_rows, PIECE), BF16),
            vmem((slots, groups, mem_rows, PIECE), BF16),
            pltpu.SMEM((slots, groups), jnp.int32),
            dma((CHUNKS, 3)),
            dma((CHUNKS,)),
            dma((items, 2)),
            dma((items, 2, CHUNKS)),
            dma((items, 2, CHUNKS)),
            dma((items,)),
            dma((items,)),
            dma((items, CHUNKS)),
            dma((items, CHUNKS)),
            dma((items, CHUNKS)),
            dma((items, CHUNKS)),
            dma((items, CHUNKS)),
            dma((items, CHUNKS)),
            dma((items,)),
            dma((items,)),
            dma((items, 2)),
            dma((items, 2)),
            dma((items, 2)),
            dma((slots,)),
            dma((slots,)),
            dma((slots,)),
            dma((slots,)),
            pltpu.SemaphoreType.REGULAR((3,)),
        ],
        compiler_params=pltpu.CompilerParams(
            collective_id=0, has_side_effects=True, vmem_limit_bytes=63 * 1024 * 1024
        ),
    )(segments, memory, lengths, routes, gain, w_query, w_key, w_value, w_out)


def place_kernel(mem, seg, mem_out, seg_out, held, in_sem, sem):
    spots = [(kind, rnd, slot) for kind in range(2) for rnd in range(mem.shape[1]) for slot in range(mem.shape[2])]
    ins, outs = [], []
    for kind, rnd, slot in spots:
        source, target = ((mem, mem_out), (seg, seg_out))[kind]
        ins.append(pltpu.make_async_copy(source.at[0, rnd, slot], held.at[kind, rnd, slot], in_sem.at[kind, rnd, slot]))
        outs.append(pltpu.make_async_copy(held.at[kind, rnd, slot], target.at[0, rnd, slot], sem.at[kind, rnd, slot]))
    for copy in ins:
        copy.start()
    for into, out in zip(ins, outs):
        into.wait()
        out.start()
    for out in outs:
        out.wait()


def place(mem, seg):
    anywhere = pl.BlockSpec(memory_space=pl.ANY)
    states = jax.ShapeDtypeStruct(mem.shape, mem.dtype)
    return pl.pallas_call(
        place_kernel,
        out_shape=(states, states),
        in_specs=[anywhere, anywhere],
        out_specs=(anywhere, anywhere),
        scratch_shapes=[
            pltpu.VMEM((2,) + mem.shape[1:], mem.dtype),
            pltpu.SemaphoreType.DMA((2,) + mem.shape[1:3]),
            pltpu.SemaphoreType.DMA((2,) + mem.shape[1:3]),
        ],
        compiler_params=pltpu.CompilerParams(vmem_limit_bytes=16 * 1024 * 1024),
    )(mem, seg)


def per_device(segments, memory_in, seg_lengths, routes, w_query, w_key, value_weight, w_out, norm_gain):
    mem, seg = run_window(
        segments, memory_in, seg_lengths, routes, norm_gain, w_query, w_key, value_weight, w_out)
    return place(mem, seg)


def solution(mesh):
    return jax.shard_map(
        per_device,
        mesh=mesh,
        in_specs=(
            P(None, "dp", "mp", None),
            P("dp", "mp", None),
            P(None, "dp"),
            P(),
            P("phase", None, "mp"),
            P("phase", None, "mp"),
            P("phase", None, "mp"),
            P("phase", "mp", None),
            P("phase", None),
        ),
        out_specs=(P("phase", None, "dp", "mp", None), P("phase", None, "dp", "mp", None)),
        check_vma=False,
    )
```

```python
import jax
import jax.numpy as jnp
from jax import lax
from jax.experimental import pallas as pl
from jax.experimental.pallas import tpu as pltpu
from jax.sharding import PartitionSpec as P

HEAD_SIZE = 128
EPSILON = 1e-05
CHUNKS = 4
AHEAD = 4
PIECE = 128
BAND = 32
MESH = pl.DeviceIdType.MESH
F32 = jnp.float32
BF16 = jnp.bfloat16


def window_kernel(
    segments, memory, lengths, routes, gain, w_query, w_key, w_value, w_out,
    mem_out, seg_out,
    wq, wk, wv, wo, rows_in, partial, own_sum, far_sum, last_sum, scaled, squares, acc_q, acc_k, acc_v,
    queries, keys, values, attended, spread_even, spread_odd, picked, origins,
    win_sem, wo_sem, own_sem, gather_send, gather_recv, keep_send, keep_recv, far_send, far_recv, near_send, near_recv,
    mem_send, mem_recv, seg_send, seg_recv, state_send, state_recv, out_sem, route_send, route_recv, back_send, back_recv, known_sem,
):
    phase = lax.axis_index("phase")
    group = lax.axis_index("dp")
    half = lax.axis_index("mp")
    groups = lax.axis_size("dp")
    peer = 1 - half
    rounds, slots, dev_rows, width = segments.shape
    mem_rows = 2 * dev_rows
    rows = 2 * mem_rows
    items = rounds * slots
    chunk = width // CHUNKS
    first = phase == 0
    second = phase == 1
    spread = (spread_even, spread_odd)
    mem_home = pl.multiple_of(half * dev_rows, dev_rows)
    seg_home = pl.multiple_of(mem_rows + half * dev_rows, dev_rows)
    mem_peer = pl.multiple_of(peer * dev_rows, dev_rows)
    seg_peer = pl.multiple_of(mem_rows + peer * dev_rows, dev_rows)

    def columns(index):
        return pl.ds(pl.multiple_of(index * chunk, chunk), chunk)

    def arrived(ref, sem):
        pltpu.make_async_copy(ref, ref, sem).wait()

    def remote(source, target, send, recv, device):
        return pltpu.make_async_remote_copy(
            src_ref=source, dst_ref=target, send_sem=send, recv_sem=recv, device_id=device, device_id_type=MESH)

    def in_copies(index):
        depth = pl.ds(index * chunk, chunk)
        return [
            pltpu.make_async_copy(source.at[0, depth], target.at[depth], win_sem.at[index, which])
            for which, (source, target) in enumerate(((w_query, wq), (w_key, wk), (w_value, wv)))
        ]

    def wo_copy(index):
        cols = columns(index)
        return pltpu.make_async_copy(w_out.at[0, :, cols], wo.at[:, cols], wo_sem.at[index])

    def entry_source(item, kind):
        return memory.at[item] if kind == 0 else segments.at[item // slots, item % slots]

    def entry_own(item, kind):
        return pltpu.make_async_copy(
            entry_source(item, kind), rows_in.at[item, pl.ds((mem_home, seg_home)[kind], dev_rows)], own_sem.at[item, kind])

    def entry_far(item, kind, index):
        cols = pl.ds(index * chunk, chunk)
        return remote(entry_source(item, kind).at[:, cols],
                      rows_in.at[item, pl.ds((mem_home, seg_home)[kind], dev_rows), cols],
                      gather_send.at[item, kind, index], gather_recv.at[item, kind, index], (0, group, peer))

    def entry_wait(item, kind, index):
        cols = pl.ds(index * chunk, chunk)
        arrived(rows_in.at[item, pl.ds((mem_peer, seg_peer)[kind], dev_rows), cols], gather_recv.at[item, kind, index])

    def keep_copy(item):
        return remote(rows_in.at[item], rows_in.at[item], keep_send.at[item], keep_recv.at[item], (1, group, half))

    def far_copy(item, index):
        slot, cols = item % slots, columns(index)
        return remote(partial.at[slot, :, cols], far_sum.at[slot, :, cols], far_send.at[item, index],
                      far_recv.at[item, index], (1, group, peer))

    def near_copy(item, index):
        slot, cols = item % slots, columns(index)
        return remote(partial.at[slot, :, cols], own_sum.at[slot, :, cols], near_send.at[item, index],
                      near_recv.at[item, index], (1, group, half))

    def mem_all(item, index):
        slot, cols = item % slots, columns(index)
        span = pl.ds(0, mem_rows)
        return remote(partial.at[slot, span, cols], last_sum.at[item, span, cols], mem_send.at[item, index],
                      mem_recv.at[item, index], (1, group, peer))

    def mem_part(item, index):
        slot, cols = item % slots, columns(index)
        return remote(partial.at[slot, pl.ds(mem_peer, dev_rows), cols], last_sum.at[item, pl.ds(0, dev_rows), cols],
                      mem_send.at[item, index], mem_recv.at[item, index], (1, group, peer))

    def seg_part(item):
        slot = item % slots
        return remote(partial.at[slot, pl.ds(seg_peer, dev_rows)], last_sum.at[item, pl.ds(mem_rows, dev_rows)],
                      seg_send.at[item], seg_recv.at[item], (1, group, peer))

    def states(item):
        rnd, slot = item // slots, item % slots
        return ((rows_in.at[item, pl.ds(mem_home, dev_rows)], mem_out.at[0, rnd, slot]),
                (rows_in.at[item, pl.ds(seg_home, dev_rows)], seg_out.at[0, rnd, slot]))

    def state_copies(item):
        return [remote(source, target, state_send.at[item, kind], state_recv.at[item, kind], (0, group, half))
                for kind, (source, target) in enumerate(states(item))]

    def out_copy(item, kind):
        source, target = states(item)[kind]
        return pltpu.make_async_copy(source, target, out_sem.at[item, kind])

    own_piece = pl.ds(pl.multiple_of(group * PIECE, PIECE), PIECE)

    def piece_copy(slot, piece):
        return remote(rows_in.at[slot, pl.ds(0, mem_rows), pl.ds(pl.multiple_of(piece * PIECE, PIECE), PIECE)],
                      spread[slot].at[group], route_send.at[slot], route_recv.at[slot], (0, piece, half))

    def reorder(slot):
        item = slots + slot
        arrived(spread[slot], route_recv.at[slot])
        rows_in[item, pl.ds(0, mem_rows), own_piece] = spread[slot][origins[slot, group]]

        @pl.loop(1, groups)
        def _(step):
            target = (group + step) % groups
            picked[slot, target] = spread[slot][origins[slot, target]]
            remote(picked.at[slot, target], rows_in.at[item, pl.ds(0, mem_rows), own_piece],
                   back_send.at[slot], back_recv.at[slot], (0, target, half)).start()

        for index in range(CHUNKS):
            entry_far(item, 1, index).start()
        arrived(picked.at[slot, pl.ds(0, groups - 1)], back_recv.at[slot])

    barrier = pltpu.get_barrier_semaphore()

    def greet(device):
        pl.semaphore_signal(barrier, inc=1, device_id=device, device_id_type=MESH)

    greet((phase, group, peer))

    @pl.when(second)
    def _():
        greet((0, group, half))
        greet((0, group, peer))

    for index in range(AHEAD):
        for copy in in_copies(index):
            copy.start()

    plane, line, side = group // 8, group // 2 % 4, group % 2
    line_mates = [(0, group + ((line + step) % 4 - line) * 2, half) for step in range(1, 4)]
    plane_mates = [(0, group + ((plane + step) % 4 - plane) * 8, half) for step in range(1, 4)]
    side_mate = (0, group + 1 - 2 * side, half)

    def tell(index, device):
        pl.semaphore_signal(known_sem.at[index], inc=1, device_id=device, device_id_type=MESH)

    @pl.when(first)
    def _():
        for device in line_mates + plane_mates + [side_mate, (1, group, half)]:
            greet(device)
        pl.semaphore_wait(barrier, 10)

        for item in range(slots):
            for kind in range(2):
                entry_own(item, kind).start()
        for index in range(CHUNKS):
            for kind in range(2):
                entry_far(0, kind, index).start()
        for item in range(slots, items):
            entry_own(item, 1).start()
        for device in plane_mates:
            tell(0, device)

        for slot in range(slots):
            @pl.loop(0, groups)
            def _(target):
                origin = jnp.int32(0)
                for source in range(groups):
                    origin = jnp.where(routes[slot, source] == target, source, origin)
                origins[slot, target] = origin

        pl.semaphore_wait(known_sem.at[0], 3)
        tell(1, side_mate)

    @pl.when(second)
    def _():
        pl.semaphore_wait(barrier, 2)

    def project(item):
        slot = item % slots

        @pl.when(first)
        def _():
            @pl.when(item < slots)
            def _():
                entry_own(slot, 0).wait()
            entry_own(item, 1).wait()

        for index in range(CHUNKS):
            cols = pl.ds(index * chunk, chunk)

            @pl.when(first)
            def _():
                @pl.when(item < slots)
                def _():
                    entry_wait(slot, 0, index)
                entry_wait(item, 1, index)
                if index == CHUNKS // 2:
                    @pl.when(item == 0)
                    def _():
                        for other in range(1, slots):
                            for ahead in range(CHUNKS):
                                for kind in range(2):
                                    entry_far(other, kind, ahead).start()

            @pl.when(second)
            def _():
                if index == 0:
                    arrived(rows_in.at[item], keep_recv.at[item])
                arrived(own_sum.at[slot, :, cols], near_recv.at[item, index])
                arrived(far_sum.at[slot, :, cols], far_recv.at[item, index])

                @pl.loop(0, rows // BAND)
                def _(band):
                    span = pl.ds(pl.multiple_of(band * BAND, BAND), BAND)
                    total = own_sum[slot, span, cols].astype(F32) + far_sum[slot, span, cols].astype(F32)
                    rows_in[item, span, cols] = (rows_in[item, span, cols].astype(F32) + total).astype(BF16)

            gain_row = gain[:, cols].astype(F32)

            @pl.loop(0, rows // BAND)
            def _(band):
                span = pl.ds(pl.multiple_of(band * BAND, BAND), BAND)
                x = rows_in[item, span, cols].astype(F32)
                scaled[span] = (x * gain_row).astype(BF16)
                square = x * x
                lanes = square[:, :128]
                for step in range(1, chunk // 128):
                    lanes = lanes + square[:, step * 128:(step + 1) * 128]
                squares[span] = lanes if index == 0 else squares[span] + lanes

            @pl.when(item == 0)
            def _():
                for copy in in_copies(index):
                    copy.wait()
                if index + AHEAD < CHUNKS:
                    for copy in in_copies(index + AHEAD):
                        copy.start()
                else:
                    for other in range(CHUNKS // AHEAD):
                        wo_copy((index + AHEAD - CHUNKS) * (CHUNKS // AHEAD) + other).start()

            depth = pl.ds(index * chunk, chunk)
            for weights, acc in ((wq, acc_q), (wk, acc_k), (wv, acc_v)):
                for start in range(0, weights.shape[1], 512):
                    part = pl.ds(start, 512)
                    product = jnp.dot(scaled[...], weights[depth, part], preferred_element_type=F32)
                    acc[:, part] = product if index == 0 else acc[:, part] + product

        @pl.when(first)
        def _():
            keep_copy(item).start()

        @pl.when(second)
        def _():
            for copy in state_copies(item):
                copy.start()

        @pl.loop(0, rows // BAND)
        def _(band):
            span = pl.ds(pl.multiple_of(band * BAND, BAND), BAND)
            factor = lax.rsqrt(jnp.sum(squares[span], axis=-1, keepdims=True) * (1.0 / width) + EPSILON)
            queries[span] = (acc_q[span] * factor).astype(BF16)
            keys[span] = (acc_k[span] * factor).astype(BF16)
            values[span] = (acc_v[span] * factor).astype(BF16)

    def attend(item):
        length = lengths[item // slots, item % slots]
        query_pos = lax.broadcasted_iota(jnp.int32, (rows, rows), 0)
        key_pos = lax.broadcasted_iota(jnp.int32, (rows, rows), 1)
        visible = (key_pos < mem_rows) | (key_pos - mem_rows < length) & (
            (query_pos < mem_rows) | (key_pos <= query_pos))
        heads = wq.shape[1] // HEAD_SIZE
        kv_heads = wk.shape[1] // HEAD_SIZE
        per = heads // kv_heads
        seen = jnp.concatenate([visible] * per, axis=0)
        for kv in range(kv_heads):
            k = keys[:, kv * HEAD_SIZE:(kv + 1) * HEAD_SIZE]
            v = values[:, kv * HEAD_SIZE:(kv + 1) * HEAD_SIZE]
            q = jnp.concatenate(
                [queries[:, head * HEAD_SIZE:(head + 1) * HEAD_SIZE] for head in range(kv * per, (kv + 1) * per)], axis=0)
            scores = lax.dot_general(q, k, (((1,), (1,)), ((), ())), preferred_element_type=F32)
            scores = jnp.where(seen, scores * HEAD_SIZE ** (-0.5), -1e30)
            weights = jnp.exp(scores - jnp.max(scores, axis=-1, keepdims=True))
            attn = (weights * (1.0 / jnp.sum(weights, axis=-1, keepdims=True))).astype(BF16)
            mixed = jnp.dot(attn, v, preferred_element_type=F32).astype(BF16)
            for step in range(per):
                head = kv * per + step
                attended[:, head * HEAD_SIZE:(head + 1) * HEAD_SIZE] = mixed[step * rows:(step + 1) * rows]

    def emit(item):
        slot = item % slots
        last = item >= items - slots

        @pl.when(item >= slots)
        def _():
            before = item - slots

            @pl.when(first)
            def _():
                for index in range(CHUNKS):
                    far_copy(before, index).wait_send()
                    near_copy(before, index).wait_send()

            @pl.when(second)
            def _():
                for index in range(CHUNKS):
                    mem_all(before, index).wait_send()
                seg_part(before).wait_send()

        for index in range(CHUNKS):
            cols = pl.ds(index * chunk, chunk)

            @pl.when(item == 0)
            def _():
                wo_copy(index).wait()

            partial[slot, :, cols] = jnp.dot(attended[...], wo[:, cols], preferred_element_type=F32).astype(BF16)

            @pl.when(first)
            def _():
                far_copy(item, index).start()
                near_copy(item, index).start()

            @pl.when(second & jnp.logical_not(last))
            def _():
                mem_all(item, index).start()

            @pl.when(second & last)
            def _():
                mem_part(item, index).start()

        @pl.when(second)
        def _():
            seg_part(item).start()

    def add_rows(item, cols, start, landed, count):
        slot = item % slots

        @pl.loop(0, count // BAND)
        def _(band):
            span = pl.ds(pl.multiple_of(start + band * BAND, BAND), BAND)
            there = pl.ds(pl.multiple_of(landed + band * BAND, BAND), BAND)
            total = partial[slot, span, cols].astype(F32) + last_sum[item, there, cols].astype(F32)
            rows_in[item, span, cols] = (rows_in[item, span, cols].astype(F32) + total).astype(BF16)

    def finish_memory(item, slot):
        state = state_copies(item)
        for copy in state:
            copy.wait_send()

        @pl.when(item < items - slots)
        def _():
            if slot == 0:
                pl.semaphore_wait(known_sem.at[2], 1)

            @pl.loop(0, CHUNKS)
            def _(index):
                cols = columns(index)
                arrived(last_sum.at[item, pl.ds(0, mem_rows), cols], mem_recv.at[item, index])
                add_rows(item, cols, 0, 0, mem_rows)

                @pl.loop(0, groups // CHUNKS)
                def _(step):
                    piece_copy(slot, index * (groups // CHUNKS) + step).start()

        @pl.when(item >= items - slots)
        def _():
            @pl.loop(0, CHUNKS)
            def _(index):
                cols = columns(index)
                arrived(last_sum.at[item, pl.ds(0, dev_rows), cols], mem_recv.at[item, index])
                add_rows(item, cols, mem_home, 0, dev_rows)

        out_copy(item, 0).start()

    def finish_segment(item):
        arrived(last_sum.at[item, pl.ds(mem_rows, dev_rows)], seg_recv.at[item])

        @pl.loop(0, CHUNKS)
        def _(index):
            add_rows(item, columns(index), seg_home, mem_rows, dev_rows)

        out_copy(item, 1).start()

    @pl.loop(0, items)
    def _(item):
        @pl.when(first & (item == slots))
        def _():
            reorder(0)

        @pl.when(first & (item == slots + 1))
        def _():
            reorder(1)

        project(item)

        @pl.when(first & (item == 0))
        def _():
            pl.semaphore_wait(known_sem.at[1], 1)
            tell(2, (1, group, half))

        @pl.when(second & (item % slots == 1))
        def _():
            finish_memory(item - 1, 0)

        attend(item)
        emit(item)

        @pl.when(second & (item % slots == 1))
        def _():
            finish_memory(item, 1)
            finish_segment(item - 1)
            finish_segment(item)

    @pl.loop(0, items)
    def _(item):
        last = item >= items - slots

        @pl.when(first)
        def _():
            for source, target in states(item)[:1]:
                arrived(target, state_recv.at[item, 0])
            for source, target in states(item)[1:]:
                arrived(target, state_recv.at[item, 1])
            for index in range(CHUNKS):
                entry_far(item, 1, index).wait_send()
            keep_copy(item).wait_send()

            @pl.when(last)
            def _():
                for index in range(CHUNKS):
                    far_copy(item, index).wait_send()
                    near_copy(item, index).wait_send()

        @pl.when(second)
        def _():
            out_copy(item, 0).wait()
            out_copy(item, 1).wait()

            @pl.when(last)
            def _():
                for index in range(CHUNKS):
                    mem_part(item, index).wait_send()
                seg_part(item).wait_send()

    for slot in range(slots):
        @pl.when(first)
        def _():
            for index in range(CHUNKS):
                entry_far(slot, 0, index).wait_send()
            arrived(picked.at[slot, pl.ds(0, groups - 1)], back_send.at[slot])

        @pl.when(second)
        def _():
            arrived(spread[slot], route_send.at[slot])


def run_window(segments, memory, lengths, routes, gain, w_query, w_key, w_value, w_out):
    rounds, slots, dev_rows, width = segments.shape
    items = rounds * slots
    mem_rows = 2 * dev_rows
    rows = 2 * mem_rows
    groups = width // PIECE
    dma = pltpu.SemaphoreType.DMA
    vmem = pltpu.VMEM
    states = jax.ShapeDtypeStruct((1, rounds, slots, dev_rows, width), BF16)
    q_width, kv_width = w_query.shape[2], w_key.shape[2]
    return pl.pallas_call(
        window_kernel,
        out_shape=(states, states),
        in_specs=[pl.BlockSpec(memory_space=pl.ANY)] * 2
        + [pl.BlockSpec(memory_space=pltpu.SMEM)] * 2
        + [pl.BlockSpec(memory_space=vmem)]
        + [pl.BlockSpec(memory_space=pl.ANY)] * 4,
        out_specs=(pl.BlockSpec(memory_space=pl.ANY), pl.BlockSpec(memory_space=pl.ANY)),
        scratch_shapes=[
            vmem(w_query.shape[1:], BF16),
            vmem(w_key.shape[1:], BF16),
            vmem(w_value.shape[1:], BF16),
            vmem(w_out.shape[1:], BF16),
            vmem((items, rows, width), BF16),
            vmem((slots, rows, width), BF16),
            vmem((slots, rows, width), BF16),
            vmem((slots, rows, width), BF16),
            vmem((items, mem_rows + dev_rows, width), BF16),
            vmem((rows, width // CHUNKS), BF16),
            vmem((rows, 128), F32),
            vmem((rows, q_width), F32),
            vmem((rows, kv_width), F32),
            vmem((rows, kv_width), F32),
            vmem((rows, q_width), BF16),
            vmem((rows, kv_width), BF16),
            vmem((rows, kv_width), BF16),
            vmem((rows, q_width), BF16),
            vmem((groups, mem_rows, PIECE), BF16),
            vmem((groups, mem_rows, PIECE), BF16),
            vmem((slots, groups, mem_rows, PIECE), BF16),
            pltpu.SMEM((slots, groups), jnp.int32),
            dma((CHUNKS, 3)),
            dma((CHUNKS,)),
            dma((items, 2)),
            dma((items, 2, CHUNKS)),
            dma((items, 2, CHUNKS)),
            dma((items,)),
            dma((items,)),
            dma((items, CHUNKS)),
            dma((items, CHUNKS)),
            dma((items, CHUNKS)),
            dma((items, CHUNKS)),
            dma((items, CHUNKS)),
            dma((items, CHUNKS)),
            dma((items,)),
            dma((items,)),
            dma((items, 2)),
            dma((items, 2)),
            dma((items, 2)),
            dma((slots,)),
            dma((slots,)),
            dma((slots,)),
            dma((slots,)),
            pltpu.SemaphoreType.REGULAR((3,)),
        ],
        compiler_params=pltpu.CompilerParams(
            collective_id=0, has_side_effects=True, vmem_limit_bytes=63 * 1024 * 1024
        ),
    )(segments, memory, lengths, routes, gain, w_query, w_key, w_value, w_out)


def place_kernel(mem, seg, mem_out, seg_out, held, in_sem, sem):
    spots = [(kind, rnd, slot) for kind in range(2) for rnd in range(mem.shape[1]) for slot in range(mem.shape[2])]
    ins, outs = [], []
    for kind, rnd, slot in spots:
        source, target = ((mem, mem_out), (seg, seg_out))[kind]
        ins.append(pltpu.make_async_copy(source.at[0, rnd, slot], held.at[kind, rnd, slot], in_sem.at[kind, rnd, slot]))
        outs.append(pltpu.make_async_copy(held.at[kind, rnd, slot], target.at[0, rnd, slot], sem.at[kind, rnd, slot]))
    for copy in ins:
        copy.start()
    for into, out in zip(ins, outs):
        into.wait()
        out.start()
    for out in outs:
        out.wait()


def place(mem, seg):
    anywhere = pl.BlockSpec(memory_space=pl.ANY)
    states = jax.ShapeDtypeStruct(mem.shape, mem.dtype)
    return pl.pallas_call(
        place_kernel,
        out_shape=(states, states),
        in_specs=[anywhere, anywhere],
        out_specs=(anywhere, anywhere),
        scratch_shapes=[
            pltpu.VMEM((2,) + mem.shape[1:], mem.dtype),
            pltpu.SemaphoreType.DMA((2,) + mem.shape[1:3]),
            pltpu.SemaphoreType.DMA((2,) + mem.shape[1:3]),
        ],
        compiler_params=pltpu.CompilerParams(vmem_limit_bytes=63 * 1024 * 1024),
    )(mem, seg)


def per_device(segments, memory_in, seg_lengths, routes, w_query, w_key, value_weight, w_out, norm_gain):
    mem, seg = run_window(
        segments, memory_in, seg_lengths, routes, norm_gain, w_query, w_key, value_weight, w_out)
    return place(mem, seg)


def solution(mesh):
    return jax.shard_map(
        per_device,
        mesh=mesh,
        in_specs=(
            P(None, "dp", "mp", None),
            P("dp", "mp", None),
            P(None, "dp"),
            P(),
            P("phase", None, "mp"),
            P("phase", None, "mp"),
            P("phase", None, "mp"),
            P("phase", "mp", None),
            P("phase", None),
        ),
        out_specs=(P("phase", None, "dp", "mp", None), P("phase", None, "dp", "mp", None)),
        check_vma=False,
    )
```

```python
import jax
import jax.numpy as jnp
from jax import lax
from jax.experimental import pallas as pl
from jax.experimental.pallas import tpu as pltpu
from jax.sharding import PartitionSpec as P

HEAD_SIZE = 128
EPSILON = 1e-05
CHUNKS = 4
AHEAD = 4
PIECE = 128
BAND = 32
MESH = pl.DeviceIdType.MESH
F32 = jnp.float32
BF16 = jnp.bfloat16


def window_kernel(
    segments, memory, lengths, routes, gain, w_query, w_key, w_value, w_out,
    mem_out, seg_out,
    wq, wk, wv, wo, rows_in, partial, own_sum, far_sum, last_sum, scaled, squares, acc_q, acc_k, acc_v,
    queries, keys, values, attended, spread_even, spread_odd, picked, origins,
    win_sem, wo_sem, own_sem, gather_send, gather_recv, keep_send, keep_recv, far_send, far_recv, near_send, near_recv,
    mem_send, mem_recv, seg_send, seg_recv, state_send, state_recv, out_sem, route_send, route_recv, back_send, back_recv, known_sem,
):
    phase = lax.axis_index("phase")
    group = lax.axis_index("dp")
    half = lax.axis_index("mp")
    groups = lax.axis_size("dp")
    peer = 1 - half
    rounds, slots, dev_rows, width = segments.shape
    mem_rows = 2 * dev_rows
    rows = 2 * mem_rows
    items = rounds * slots
    chunk = width // CHUNKS
    first = phase == 0
    second = phase == 1
    spread = (spread_even, spread_odd)
    mem_home = pl.multiple_of(half * dev_rows, dev_rows)
    seg_home = pl.multiple_of(mem_rows + half * dev_rows, dev_rows)
    mem_peer = pl.multiple_of(peer * dev_rows, dev_rows)
    seg_peer = pl.multiple_of(mem_rows + peer * dev_rows, dev_rows)

    def columns(index):
        return pl.ds(pl.multiple_of(index * chunk, chunk), chunk)

    def arrived(ref, sem):
        pltpu.make_async_copy(ref, ref, sem).wait()

    def remote(source, target, send, recv, device):
        return pltpu.make_async_remote_copy(
            src_ref=source, dst_ref=target, send_sem=send, recv_sem=recv, device_id=device, device_id_type=MESH)

    def in_copies(index):
        depth = pl.ds(index * chunk, chunk)
        return [
            pltpu.make_async_copy(source.at[0, depth], target.at[depth], win_sem.at[index, which])
            for which, (source, target) in enumerate(((w_query, wq), (w_key, wk), (w_value, wv)))
        ]

    def wo_copy(index):
        cols = columns(index)
        return pltpu.make_async_copy(w_out.at[0, :, cols], wo.at[:, cols], wo_sem.at[index])

    def entry_source(item, kind):
        return memory.at[item] if kind == 0 else segments.at[item // slots, item % slots]

    def entry_own(item, kind):
        return pltpu.make_async_copy(
            entry_source(item, kind), rows_in.at[item, pl.ds((mem_home, seg_home)[kind], dev_rows)], own_sem.at[item, kind])

    def entry_far(item, kind, index):
        cols = pl.ds(index * chunk, chunk)
        return remote(entry_source(item, kind).at[:, cols],
                      rows_in.at[item, pl.ds((mem_home, seg_home)[kind], dev_rows), cols],
                      gather_send.at[item, kind, index], gather_recv.at[item, kind, index], (0, group, peer))

    def entry_wait(item, kind, index):
        cols = pl.ds(index * chunk, chunk)
        arrived(rows_in.at[item, pl.ds((mem_peer, seg_peer)[kind], dev_rows), cols], gather_recv.at[item, kind, index])

    def keep_copy(item):
        return remote(rows_in.at[item], rows_in.at[item], keep_send.at[item], keep_recv.at[item], (1, group, half))

    def far_copy(item, index):
        slot, cols = item % slots, columns(index)
        return remote(partial.at[slot, :, cols], far_sum.at[slot, :, cols], far_send.at[item, index],
                      far_recv.at[item, index], (1, group, peer))

    def near_copy(item, index):
        slot, cols = item % slots, columns(index)
        return remote(partial.at[slot, :, cols], own_sum.at[slot, :, cols], near_send.at[item, index],
                      near_recv.at[item, index], (1, group, half))

    def mem_all(item, index):
        slot, cols = item % slots, columns(index)
        span = pl.ds(0, mem_rows)
        return remote(partial.at[slot, span, cols], last_sum.at[item, span, cols], mem_send.at[item, index],
                      mem_recv.at[item, index], (1, group, peer))

    def mem_part(item, index):
        slot, cols = item % slots, columns(index)
        return remote(partial.at[slot, pl.ds(mem_peer, dev_rows), cols], last_sum.at[item, pl.ds(0, dev_rows), cols],
                      mem_send.at[item, index], mem_recv.at[item, index], (1, group, peer))

    def seg_part(item):
        slot = item % slots
        return remote(partial.at[slot, pl.ds(seg_peer, dev_rows)], last_sum.at[item, pl.ds(mem_rows, dev_rows)],
                      seg_send.at[item], seg_recv.at[item], (1, group, peer))

    def states(item):
        rnd, slot = item // slots, item % slots
        return ((rows_in.at[item, pl.ds(mem_home, dev_rows)], mem_out.at[0, rnd, slot]),
                (rows_in.at[item, pl.ds(seg_home, dev_rows)], seg_out.at[0, rnd, slot]))

    def state_copies(item):
        return [remote(source, target, state_send.at[item, kind], state_recv.at[item, kind], (0, group, half))
                for kind, (source, target) in enumerate(states(item))]

    def out_copy(item, kind):
        source, target = states(item)[kind]
        return pltpu.make_async_copy(source, target, out_sem.at[item, kind])

    own_piece = pl.ds(pl.multiple_of(group * PIECE, PIECE), PIECE)

    def piece_copy(slot, piece):
        return remote(rows_in.at[slot, pl.ds(0, mem_rows), pl.ds(pl.multiple_of(piece * PIECE, PIECE), PIECE)],
                      spread[slot].at[group], route_send.at[slot], route_recv.at[slot], (0, piece, half))

    def reorder(slot):
        item = slots + slot
        arrived(spread[slot], route_recv.at[slot])
        rows_in[item, pl.ds(0, mem_rows), own_piece] = spread[slot][origins[slot, group]]

        @pl.loop(1, groups)
        def _(step):
            target = (group + step) % groups
            picked[slot, target] = spread[slot][origins[slot, target]]
            remote(picked.at[slot, target], rows_in.at[item, pl.ds(0, mem_rows), own_piece],
                   back_send.at[slot], back_recv.at[slot], (0, target, half)).start()

        for index in range(CHUNKS):
            entry_far(item, 1, index).start()
        arrived(picked.at[slot, pl.ds(0, groups - 1)], back_recv.at[slot])

    barrier = pltpu.get_barrier_semaphore()

    def greet(device):
        pl.semaphore_signal(barrier, inc=1, device_id=device, device_id_type=MESH)

    greet((phase, group, peer))

    @pl.when(second)
    def _():
        greet((0, group, half))
        greet((0, group, peer))

    for index in range(AHEAD):
        for copy in in_copies(index):
            copy.start()

    plane, line, side = group // 8, group // 2 % 4, group % 2
    line_mates = [(0, group + ((line + step) % 4 - line) * 2, half) for step in range(1, 4)]
    plane_mates = [(0, group + ((plane + step) % 4 - plane) * 8, half) for step in range(1, 4)]
    side_mate = (0, group + 1 - 2 * side, half)

    def tell(index, device):
        pl.semaphore_signal(known_sem.at[index], inc=1, device_id=device, device_id_type=MESH)

    @pl.when(first)
    def _():
        for device in line_mates + plane_mates + [side_mate, (1, group, half)]:
            greet(device)
        pl.semaphore_wait(barrier, 10)

        for item in range(slots):
            for kind in range(2):
                entry_own(item, kind).start()
        for index in range(CHUNKS):
            for kind in range(2):
                entry_far(0, kind, index).start()
        for item in range(slots, items):
            entry_own(item, 1).start()
        for device in plane_mates:
            tell(0, device)

        for slot in range(slots):
            @pl.loop(0, groups)
            def _(target):
                origin = jnp.int32(0)
                for source in range(groups):
                    origin = jnp.where(routes[slot, source] == target, source, origin)
                origins[slot, target] = origin

        pl.semaphore_wait(known_sem.at[0], 3)
        tell(1, side_mate)

    @pl.when(second)
    def _():
        pl.semaphore_wait(barrier, 2)

    def project(item):
        slot = item % slots

        @pl.when(first)
        def _():
            @pl.when(item < slots)
            def _():
                entry_own(slot, 0).wait()
            entry_own(item, 1).wait()

        for index in range(CHUNKS):
            cols = pl.ds(index * chunk, chunk)

            @pl.when(first)
            def _():
                @pl.when(item < slots)
                def _():
                    entry_wait(slot, 0, index)
                entry_wait(item, 1, index)
                if index == CHUNKS // 2:
                    @pl.when(item == 0)
                    def _():
                        for other in range(1, slots):
                            for ahead in range(CHUNKS):
                                for kind in range(2):
                                    entry_far(other, kind, ahead).start()

            @pl.when(second)
            def _():
                if index == 0:
                    arrived(rows_in.at[item], keep_recv.at[item])
                arrived(own_sum.at[slot, :, cols], near_recv.at[item, index])
                arrived(far_sum.at[slot, :, cols], far_recv.at[item, index])

                @pl.loop(0, rows // BAND)
                def _(band):
                    span = pl.ds(pl.multiple_of(band * BAND, BAND), BAND)
                    total = own_sum[slot, span, cols].astype(F32) + far_sum[slot, span, cols].astype(F32)
                    rows_in[item, span, cols] = (rows_in[item, span, cols].astype(F32) + total).astype(BF16)

            gain_row = gain[:, cols].astype(F32)

            @pl.loop(0, rows // BAND)
            def _(band):
                span = pl.ds(pl.multiple_of(band * BAND, BAND), BAND)
                x = rows_in[item, span, cols].astype(F32)
                scaled[span] = (x * gain_row).astype(BF16)
                square = x * x
                lanes = square[:, :128]
                for step in range(1, chunk // 128):
                    lanes = lanes + square[:, step * 128:(step + 1) * 128]
                squares[span] = lanes if index == 0 else squares[span] + lanes

            @pl.when(item == 0)
            def _():
                for copy in in_copies(index):
                    copy.wait()
                if index + AHEAD < CHUNKS:
                    for copy in in_copies(index + AHEAD):
                        copy.start()
                else:
                    for other in range(CHUNKS // AHEAD):
                        wo_copy((index + AHEAD - CHUNKS) * (CHUNKS // AHEAD) + other).start()

            depth = pl.ds(index * chunk, chunk)
            for weights, acc in ((wq, acc_q), (wk, acc_k), (wv, acc_v)):
                for start in range(0, weights.shape[1], 512):
                    part = pl.ds(start, 512)
                    product = jnp.dot(scaled[...], weights[depth, part], preferred_element_type=F32)
                    acc[:, part] = product if index == 0 else acc[:, part] + product

        @pl.when(first)
        def _():
            keep_copy(item).start()

        @pl.when(second)
        def _():
            for copy in state_copies(item):
                copy.start()

        @pl.loop(0, rows // BAND)
        def _(band):
            span = pl.ds(pl.multiple_of(band * BAND, BAND), BAND)
            factor = lax.rsqrt(jnp.sum(squares[span], axis=-1, keepdims=True) * (1.0 / width) + EPSILON)
            queries[span] = (acc_q[span] * factor).astype(BF16)
            keys[span] = (acc_k[span] * factor).astype(BF16)
            values[span] = (acc_v[span] * factor).astype(BF16)

    def attend(item):
        length = lengths[item // slots, item % slots]
        query_pos = lax.broadcasted_iota(jnp.int32, (rows, rows), 0)
        key_pos = lax.broadcasted_iota(jnp.int32, (rows, rows), 1)
        visible = (key_pos < mem_rows) | (key_pos - mem_rows < length) & (
            (query_pos < mem_rows) | (key_pos <= query_pos))
        heads = wq.shape[1] // HEAD_SIZE
        kv_heads = wk.shape[1] // HEAD_SIZE
        per = heads // kv_heads
        seen = jnp.concatenate([visible] * per, axis=0)
        for kv in range(kv_heads):
            k = keys[:, kv * HEAD_SIZE:(kv + 1) * HEAD_SIZE]
            v = values[:, kv * HEAD_SIZE:(kv + 1) * HEAD_SIZE]
            q = jnp.concatenate(
                [queries[:, head * HEAD_SIZE:(head + 1) * HEAD_SIZE] for head in range(kv * per, (kv + 1) * per)], axis=0)
            scores = lax.dot_general(q, k, (((1,), (1,)), ((), ())), preferred_element_type=F32)
            scores = jnp.where(seen, scores * HEAD_SIZE ** (-0.5), -1e30)
            weights = jnp.exp(scores - jnp.max(scores, axis=-1, keepdims=True))
            attn = (weights * (1.0 / jnp.sum(weights, axis=-1, keepdims=True))).astype(BF16)
            mixed = jnp.dot(attn, v, preferred_element_type=F32).astype(BF16)
            for step in range(per):
                head = kv * per + step
                attended[:, head * HEAD_SIZE:(head + 1) * HEAD_SIZE] = mixed[step * rows:(step + 1) * rows]

    def emit(item):
        slot = item % slots
        last = item >= items - slots

        @pl.when(item >= slots)
        def _():
            before = item - slots

            @pl.when(first)
            def _():
                for index in range(CHUNKS):
                    far_copy(before, index).wait_send()
                    near_copy(before, index).wait_send()

            @pl.when(second)
            def _():
                for index in range(CHUNKS):
                    mem_all(before, index).wait_send()
                seg_part(before).wait_send()

        for index in range(CHUNKS):
            cols = pl.ds(index * chunk, chunk)

            @pl.when(item == 0)
            def _():
                wo_copy(index).wait()

            partial[slot, :, cols] = jnp.dot(attended[...], wo[:, cols], preferred_element_type=F32).astype(BF16)

            @pl.when(first)
            def _():
                far_copy(item, index).start()
                near_copy(item, index).start()

            @pl.when(second & jnp.logical_not(last))
            def _():
                mem_all(item, index).start()

            @pl.when(second & last)
            def _():
                mem_part(item, index).start()

        @pl.when(second & last)
        def _():
            seg_part(item).start()

    def add_rows(item, cols, start, landed, count):
        slot = item % slots

        @pl.loop(0, count // BAND)
        def _(band):
            span = pl.ds(pl.multiple_of(start + band * BAND, BAND), BAND)
            there = pl.ds(pl.multiple_of(landed + band * BAND, BAND), BAND)
            total = partial[slot, span, cols].astype(F32) + last_sum[item, there, cols].astype(F32)
            rows_in[item, span, cols] = (rows_in[item, span, cols].astype(F32) + total).astype(BF16)

    def finish_memory(item, slot):
        state = state_copies(item)
        for copy in state:
            copy.wait_send()

        @pl.when(item < items - slots)
        def _():
            if slot == 0:
                pl.semaphore_wait(known_sem.at[2], 1)

            @pl.loop(0, CHUNKS)
            def _(index):
                cols = columns(index)
                arrived(last_sum.at[item, pl.ds(0, mem_rows), cols], mem_recv.at[item, index])
                add_rows(item, cols, 0, 0, mem_rows)

                @pl.loop(0, groups // CHUNKS)
                def _(step):
                    piece_copy(slot, index * (groups // CHUNKS) + step).start()

        @pl.when(item >= items - slots)
        def _():
            @pl.loop(0, CHUNKS)
            def _(index):
                cols = columns(index)
                arrived(last_sum.at[item, pl.ds(0, dev_rows), cols], mem_recv.at[item, index])
                add_rows(item, cols, mem_home, 0, dev_rows)

        out_copy(item, 0).start()

    def finish_segment(item):
        arrived(last_sum.at[item, pl.ds(mem_rows, dev_rows)], seg_recv.at[item])

        @pl.loop(0, CHUNKS)
        def _(index):
            add_rows(item, columns(index), seg_home, mem_rows, dev_rows)

        out_copy(item, 1).start()

    @pl.loop(0, items)
    def _(item):
        @pl.when(first & (item == slots))
        def _():
            reorder(0)

        @pl.when(first & (item == slots + 1))
        def _():
            reorder(1)

        @pl.when(second & (item == 1))
        def _():
            finish_memory(item - 1, 0)

        project(item)

        @pl.when(first & (item == 0))
        def _():
            pl.semaphore_wait(known_sem.at[1], 1)
            tell(2, (1, group, half))

        attend(item)
        emit(item)

        @pl.when(second & (item == items - 1))
        def _():
            finish_memory(item - 1, 0)

        @pl.when(second & (item % slots == 1))
        def _():
            finish_memory(item, 1)

            @pl.when(item < items - slots)
            def _():
                seg_part(item - 1).start()
                seg_part(item).start()

            finish_segment(item - 1)
            finish_segment(item)

    @pl.loop(0, items)
    def _(item):
        last = item >= items - slots

        @pl.when(first)
        def _():
            for source, target in states(item)[:1]:
                arrived(target, state_recv.at[item, 0])
            for source, target in states(item)[1:]:
                arrived(target, state_recv.at[item, 1])
            for index in range(CHUNKS):
                entry_far(item, 1, index).wait_send()
            keep_copy(item).wait_send()

            @pl.when(last)
            def _():
                for index in range(CHUNKS):
                    far_copy(item, index).wait_send()
                    near_copy(item, index).wait_send()

        @pl.when(second)
        def _():
            out_copy(item, 0).wait()
            out_copy(item, 1).wait()

            @pl.when(last)
            def _():
                for index in range(CHUNKS):
                    mem_part(item, index).wait_send()
                seg_part(item).wait_send()

    for slot in range(slots):
        @pl.when(first)
        def _():
            for index in range(CHUNKS):
                entry_far(slot, 0, index).wait_send()
            arrived(picked.at[slot, pl.ds(0, groups - 1)], back_send.at[slot])

        @pl.when(second)
        def _():
            arrived(spread[slot], route_send.at[slot])


def run_window(segments, memory, lengths, routes, gain, w_query, w_key, w_value, w_out):
    rounds, slots, dev_rows, width = segments.shape
    items = rounds * slots
    mem_rows = 2 * dev_rows
    rows = 2 * mem_rows
    groups = width // PIECE
    dma = pltpu.SemaphoreType.DMA
    vmem = pltpu.VMEM
    states = jax.ShapeDtypeStruct((1, rounds, slots, dev_rows, width), BF16)
    q_width, kv_width = w_query.shape[2], w_key.shape[2]
    return pl.pallas_call(
        window_kernel,
        out_shape=(states, states),
        in_specs=[pl.BlockSpec(memory_space=pl.ANY)] * 2
        + [pl.BlockSpec(memory_space=pltpu.SMEM)] * 2
        + [pl.BlockSpec(memory_space=vmem)]
        + [pl.BlockSpec(memory_space=pl.ANY)] * 4,
        out_specs=(pl.BlockSpec(memory_space=pl.ANY), pl.BlockSpec(memory_space=pl.ANY)),
        scratch_shapes=[
            vmem(w_query.shape[1:], BF16),
            vmem(w_key.shape[1:], BF16),
            vmem(w_value.shape[1:], BF16),
            vmem(w_out.shape[1:], BF16),
            vmem((items, rows, width), BF16),
            vmem((slots, rows, width), BF16),
            vmem((slots, rows, width), BF16),
            vmem((slots, rows, width), BF16),
            vmem((items, mem_rows + dev_rows, width), BF16),
            vmem((rows, width // CHUNKS), BF16),
            vmem((rows, 128), F32),
            vmem((rows, q_width), F32),
            vmem((rows, kv_width), F32),
            vmem((rows, kv_width), F32),
            vmem((rows, q_width), BF16),
            vmem((rows, kv_width), BF16),
            vmem((rows, kv_width), BF16),
            vmem((rows, q_width), BF16),
            vmem((groups, mem_rows, PIECE), BF16),
            vmem((groups, mem_rows, PIECE), BF16),
            vmem((slots, groups, mem_rows, PIECE), BF16),
            pltpu.SMEM((slots, groups), jnp.int32),
            dma((CHUNKS, 3)),
            dma((CHUNKS,)),
            dma((items, 2)),
            dma((items, 2, CHUNKS)),
            dma((items, 2, CHUNKS)),
            dma((items,)),
            dma((items,)),
            dma((items, CHUNKS)),
            dma((items, CHUNKS)),
            dma((items, CHUNKS)),
            dma((items, CHUNKS)),
            dma((items, CHUNKS)),
            dma((items, CHUNKS)),
            dma((items,)),
            dma((items,)),
            dma((items, 2)),
            dma((items, 2)),
            dma((items, 2)),
            dma((slots,)),
            dma((slots,)),
            dma((slots,)),
            dma((slots,)),
            pltpu.SemaphoreType.REGULAR((3,)),
        ],
        compiler_params=pltpu.CompilerParams(
            collective_id=0, has_side_effects=True, vmem_limit_bytes=63 * 1024 * 1024
        ),
    )(segments, memory, lengths, routes, gain, w_query, w_key, w_value, w_out)


def place_kernel(mem, seg, mem_out, seg_out, held, in_sem, sem):
    spots = [(kind, rnd, slot) for kind in range(2) for rnd in range(mem.shape[1]) for slot in range(mem.shape[2])]
    ins, outs = [], []
    for kind, rnd, slot in spots:
        source, target = ((mem, mem_out), (seg, seg_out))[kind]
        ins.append(pltpu.make_async_copy(source.at[0, rnd, slot], held.at[kind, rnd, slot], in_sem.at[kind, rnd, slot]))
        outs.append(pltpu.make_async_copy(held.at[kind, rnd, slot], target.at[0, rnd, slot], sem.at[kind, rnd, slot]))
    for copy in ins:
        copy.start()
    for into, out in zip(ins, outs):
        into.wait()
        out.start()
    for out in outs:
        out.wait()


def place(mem, seg):
    anywhere = pl.BlockSpec(memory_space=pl.ANY)
    states = jax.ShapeDtypeStruct(mem.shape, mem.dtype)
    return pl.pallas_call(
        place_kernel,
        out_shape=(states, states),
        in_specs=[anywhere, anywhere],
        out_specs=(anywhere, anywhere),
        scratch_shapes=[
            pltpu.VMEM((2,) + mem.shape[1:], mem.dtype),
            pltpu.SemaphoreType.DMA((2,) + mem.shape[1:3]),
            pltpu.SemaphoreType.DMA((2,) + mem.shape[1:3]),
        ],
        compiler_params=pltpu.CompilerParams(vmem_limit_bytes=63 * 1024 * 1024),
    )(mem, seg)


def per_device(segments, memory_in, seg_lengths, routes, w_query, w_key, value_weight, w_out, norm_gain):
    mem, seg = run_window(
        segments, memory_in, seg_lengths, routes, norm_gain, w_query, w_key, value_weight, w_out)
    return place(mem, seg)


def solution(mesh):
    return jax.shard_map(
        per_device,
        mesh=mesh,
        in_specs=(
            P(None, "dp", "mp", None),
            P("dp", "mp", None),
            P(None, "dp"),
            P(),
            P("phase", None, "mp"),
            P("phase", None, "mp"),
            P("phase", None, "mp"),
            P("phase", "mp", None),
            P("phase", None),
        ),
        out_specs=(P("phase", None, "dp", "mp", None), P("phase", None, "dp", "mp", None)),
        check_vma=False,
    )
```

```python
import jax
import jax.numpy as jnp
from jax import lax
from jax.experimental import pallas as pl
from jax.experimental.pallas import tpu as pltpu
from jax.sharding import PartitionSpec as P

HEAD_SIZE = 128
EPSILON = 1e-05
CHUNKS = 4
AHEAD = 4
PIECE = 128
BAND = 32
MESH = pl.DeviceIdType.MESH
F32 = jnp.float32
BF16 = jnp.bfloat16


def window_kernel(
    segments, memory, lengths, routes, gain, w_query, w_key, w_value, w_out,
    mem_out, seg_out,
    wq, wk, wv, wo, rows_in, partial, own_sum, far_sum, last_sum, scaled, squares, acc_q, acc_k, acc_v,
    queries, keys, values, attended, spread_even, spread_odd, picked, origins,
    win_sem, wo_sem, own_sem, gather_send, gather_recv, keep_send, keep_recv, far_send, far_recv, near_send, near_recv,
    mem_send, mem_recv, seg_send, seg_recv, state_send, state_recv, out_sem, route_send, route_recv, back_send, back_recv, known_sem,
):
    phase = lax.axis_index("phase")
    group = lax.axis_index("dp")
    half = lax.axis_index("mp")
    groups = lax.axis_size("dp")
    peer = 1 - half
    rounds, slots, dev_rows, width = segments.shape
    mem_rows = 2 * dev_rows
    rows = 2 * mem_rows
    items = rounds * slots
    chunk = width // CHUNKS
    first = phase == 0
    second = phase == 1
    spread = (spread_even, spread_odd)
    mem_home = pl.multiple_of(half * dev_rows, dev_rows)
    seg_home = pl.multiple_of(mem_rows + half * dev_rows, dev_rows)
    mem_peer = pl.multiple_of(peer * dev_rows, dev_rows)
    seg_peer = pl.multiple_of(mem_rows + peer * dev_rows, dev_rows)

    def columns(index):
        return pl.ds(pl.multiple_of(index * chunk, chunk), chunk)

    def arrived(ref, sem):
        pltpu.make_async_copy(ref, ref, sem).wait()

    def remote(source, target, send, recv, device):
        return pltpu.make_async_remote_copy(
            src_ref=source, dst_ref=target, send_sem=send, recv_sem=recv, device_id=device, device_id_type=MESH)

    def in_copies(index):
        depth = pl.ds(index * chunk, chunk)
        return [
            pltpu.make_async_copy(source.at[0, depth], target.at[depth], win_sem.at[index, which])
            for which, (source, target) in enumerate(((w_query, wq), (w_key, wk), (w_value, wv)))
        ]

    def wo_copy(index):
        cols = columns(index)
        return pltpu.make_async_copy(w_out.at[0, :, cols], wo.at[:, cols], wo_sem.at[index])

    def entry_source(item, kind):
        return memory.at[item] if kind == 0 else segments.at[item // slots, item % slots]

    def entry_own(item, kind):
        return pltpu.make_async_copy(
            entry_source(item, kind), rows_in.at[item, pl.ds((mem_home, seg_home)[kind], dev_rows)], own_sem.at[item, kind])

    def entry_far(item, kind, index):
        cols = pl.ds(index * chunk, chunk)
        return remote(entry_source(item, kind).at[:, cols],
                      rows_in.at[item, pl.ds((mem_home, seg_home)[kind], dev_rows), cols],
                      gather_send.at[item, kind, index], gather_recv.at[item, kind, index], (0, group, peer))

    def entry_wait(item, kind, index):
        cols = pl.ds(index * chunk, chunk)
        arrived(rows_in.at[item, pl.ds((mem_peer, seg_peer)[kind], dev_rows), cols], gather_recv.at[item, kind, index])

    def keep_copy(item):
        return remote(rows_in.at[item], rows_in.at[item], keep_send.at[item], keep_recv.at[item], (1, group, half))

    def far_copy(item, index):
        slot, cols = item % slots, columns(index)
        return remote(partial.at[slot, :, cols], far_sum.at[slot, :, cols], far_send.at[item, index],
                      far_recv.at[item, index], (1, group, peer))

    def near_copy(item, index):
        slot, cols = item % slots, columns(index)
        return remote(partial.at[slot, :, cols], own_sum.at[slot, :, cols], near_send.at[item, index],
                      near_recv.at[item, index], (1, group, half))

    def mem_all(item, index):
        slot, cols = item % slots, columns(index)
        span = pl.ds(0, mem_rows)
        return remote(partial.at[slot, span, cols], last_sum.at[item, span, cols], mem_send.at[item, index],
                      mem_recv.at[item, index], (1, group, peer))

    def mem_part(item, index):
        slot, cols = item % slots, columns(index)
        return remote(partial.at[slot, pl.ds(mem_peer, dev_rows), cols], last_sum.at[item, pl.ds(0, dev_rows), cols],
                      mem_send.at[item, index], mem_recv.at[item, index], (1, group, peer))

    def seg_part(item):
        slot = item % slots
        return remote(partial.at[slot, pl.ds(seg_peer, dev_rows)], last_sum.at[item, pl.ds(mem_rows, dev_rows)],
                      seg_send.at[item], seg_recv.at[item], (1, group, peer))

    def states(item):
        rnd, slot = item // slots, item % slots
        return ((rows_in.at[item, pl.ds(mem_home, dev_rows)], mem_out.at[0, rnd, slot]),
                (rows_in.at[item, pl.ds(seg_home, dev_rows)], seg_out.at[0, rnd, slot]))

    def state_copies(item):
        return [remote(source, target, state_send.at[item, kind], state_recv.at[item, kind], (0, group, half))
                for kind, (source, target) in enumerate(states(item))]

    def out_copy(item, kind):
        source, target = states(item)[kind]
        return pltpu.make_async_copy(source, target, out_sem.at[item, kind])

    own_piece = pl.ds(pl.multiple_of(group * PIECE, PIECE), PIECE)

    def piece_copy(slot, piece):
        return remote(rows_in.at[slot, pl.ds(0, mem_rows), pl.ds(pl.multiple_of(piece * PIECE, PIECE), PIECE)],
                      spread[slot].at[group], route_send.at[slot], route_recv.at[slot], (0, piece, half))

    def reorder(slot):
        item = slots + slot
        arrived(spread[slot], route_recv.at[slot])
        rows_in[item, pl.ds(0, mem_rows), own_piece] = spread[slot][origins[slot, group]]

        @pl.loop(1, groups)
        def _(step):
            target = (group + step) % groups
            picked[slot, target] = spread[slot][origins[slot, target]]
            remote(picked.at[slot, target], rows_in.at[item, pl.ds(0, mem_rows), own_piece],
                   back_send.at[slot], back_recv.at[slot], (0, target, half)).start()

        for index in range(CHUNKS):
            entry_far(item, 1, index).start()
        arrived(picked.at[slot, pl.ds(0, groups - 1)], back_recv.at[slot])

    barrier = pltpu.get_barrier_semaphore()

    def greet(device):
        pl.semaphore_signal(barrier, inc=1, device_id=device, device_id_type=MESH)

    greet((phase, group, peer))

    @pl.when(second)
    def _():
        greet((0, group, half))
        greet((0, group, peer))

    for index in range(AHEAD):
        for copy in in_copies(index):
            copy.start()

    plane, line, side = group // 8, group // 2 % 4, group % 2
    line_mates = [(0, group + ((line + step) % 4 - line) * 2, half) for step in range(1, 4)]
    plane_mates = [(0, group + ((plane + step) % 4 - plane) * 8, half) for step in range(1, 4)]
    side_mate = (0, group + 1 - 2 * side, half)

    def tell(index, device):
        pl.semaphore_signal(known_sem.at[index], inc=1, device_id=device, device_id_type=MESH)

    @pl.when(first)
    def _():
        for device in line_mates + plane_mates + [side_mate, (1, group, half)]:
            greet(device)
        pl.semaphore_wait(barrier, 10)

        for item in range(slots):
            for kind in range(2):
                entry_own(item, kind).start()
        for index in range(CHUNKS):
            for kind in range(2):
                entry_far(0, kind, index).start()
        for item in range(slots, items):
            entry_own(item, 1).start()
        for device in plane_mates:
            tell(0, device)

        for slot in range(slots):
            @pl.loop(0, groups)
            def _(target):
                origin = jnp.int32(0)
                for source in range(groups):
                    origin = jnp.where(routes[slot, source] == target, source, origin)
                origins[slot, target] = origin

        pl.semaphore_wait(known_sem.at[0], 3)
        tell(1, side_mate)

    @pl.when(second)
    def _():
        pl.semaphore_wait(barrier, 2)

    def project(item):
        slot = item % slots

        @pl.when(first)
        def _():
            @pl.when(item < slots)
            def _():
                entry_own(slot, 0).wait()
            entry_own(item, 1).wait()

        for index in range(CHUNKS):
            cols = pl.ds(index * chunk, chunk)

            @pl.when(first)
            def _():
                @pl.when(item < slots)
                def _():
                    entry_wait(slot, 0, index)
                entry_wait(item, 1, index)
                if index == CHUNKS // 2:
                    @pl.when(item == 0)
                    def _():
                        for other in range(1, slots):
                            for ahead in range(CHUNKS):
                                for kind in range(2):
                                    entry_far(other, kind, ahead).start()

            @pl.when(second)
            def _():
                if index == 0:
                    arrived(rows_in.at[item], keep_recv.at[item])
                arrived(own_sum.at[slot, :, cols], near_recv.at[item, index])
                arrived(far_sum.at[slot, :, cols], far_recv.at[item, index])

                @pl.loop(0, rows // BAND)
                def _(band):
                    span = pl.ds(pl.multiple_of(band * BAND, BAND), BAND)
                    total = own_sum[slot, span, cols].astype(F32) + far_sum[slot, span, cols].astype(F32)
                    rows_in[item, span, cols] = (rows_in[item, span, cols].astype(F32) + total).astype(BF16)

            gain_row = gain[:, cols].astype(F32)

            @pl.loop(0, rows // BAND)
            def _(band):
                span = pl.ds(pl.multiple_of(band * BAND, BAND), BAND)
                x = rows_in[item, span, cols].astype(F32)
                scaled[span] = (x * gain_row).astype(BF16)
                square = x * x
                lanes = square[:, :128]
                for step in range(1, chunk // 128):
                    lanes = lanes + square[:, step * 128:(step + 1) * 128]
                squares[span] = lanes if index == 0 else squares[span] + lanes

            @pl.when(item == 0)
            def _():
                for copy in in_copies(index):
                    copy.wait()
                if index + AHEAD < CHUNKS:
                    for copy in in_copies(index + AHEAD):
                        copy.start()
                else:
                    for other in range(CHUNKS // AHEAD):
                        wo_copy((index + AHEAD - CHUNKS) * (CHUNKS // AHEAD) + other).start()

            depth = pl.ds(index * chunk, chunk)
            for weights, acc in ((wq, acc_q), (wk, acc_k), (wv, acc_v)):
                for start in range(0, weights.shape[1], 512):
                    part = pl.ds(start, 512)
                    product = jnp.dot(scaled[...], weights[depth, part], preferred_element_type=F32)
                    acc[:, part] = product if index == 0 else acc[:, part] + product

        @pl.when(first)
        def _():
            keep_copy(item).start()

        @pl.when(second)
        def _():
            for copy in state_copies(item):
                copy.start()

        @pl.loop(0, rows // BAND)
        def _(band):
            span = pl.ds(pl.multiple_of(band * BAND, BAND), BAND)
            factor = lax.rsqrt(jnp.sum(squares[span], axis=-1, keepdims=True) * (1.0 / width) + EPSILON)
            queries[span] = (acc_q[span] * factor).astype(BF16)
            keys[span] = (acc_k[span] * factor).astype(BF16)
            values[span] = (acc_v[span] * factor).astype(BF16)

    def attend(item):
        length = lengths[item // slots, item % slots]
        query_pos = lax.broadcasted_iota(jnp.int32, (rows, rows), 0)
        key_pos = lax.broadcasted_iota(jnp.int32, (rows, rows), 1)
        visible = (key_pos < mem_rows) | (key_pos - mem_rows < length) & (
            (query_pos < mem_rows) | (key_pos <= query_pos))
        heads = wq.shape[1] // HEAD_SIZE
        kv_heads = wk.shape[1] // HEAD_SIZE
        per = heads // kv_heads
        seen = jnp.concatenate([visible] * per, axis=0)
        for kv in range(kv_heads):
            k = keys[:, kv * HEAD_SIZE:(kv + 1) * HEAD_SIZE]
            v = values[:, kv * HEAD_SIZE:(kv + 1) * HEAD_SIZE]
            q = jnp.concatenate(
                [queries[:, head * HEAD_SIZE:(head + 1) * HEAD_SIZE] for head in range(kv * per, (kv + 1) * per)], axis=0)
            scores = lax.dot_general(q, k, (((1,), (1,)), ((), ())), preferred_element_type=F32)
            scores = jnp.where(seen, scores * HEAD_SIZE ** (-0.5), -1e30)
            weights = jnp.exp(scores - jnp.max(scores, axis=-1, keepdims=True))
            attn = (weights * (1.0 / jnp.sum(weights, axis=-1, keepdims=True))).astype(BF16)
            mixed = jnp.dot(attn, v, preferred_element_type=F32).astype(BF16)
            for step in range(per):
                head = kv * per + step
                attended[:, head * HEAD_SIZE:(head + 1) * HEAD_SIZE] = mixed[step * rows:(step + 1) * rows]

    def emit(item):
        slot = item % slots
        last = item >= items - slots

        @pl.when(item >= slots)
        def _():
            before = item - slots

            @pl.when(first)
            def _():
                for index in range(CHUNKS):
                    far_copy(before, index).wait_send()
                    near_copy(before, index).wait_send()

            @pl.when(second)
            def _():
                for index in range(CHUNKS):
                    mem_all(before, index).wait_send()
                seg_part(before).wait_send()

        for index in range(CHUNKS):
            cols = pl.ds(index * chunk, chunk)

            @pl.when(item == 0)
            def _():
                wo_copy(index).wait()

            partial[slot, :, cols] = jnp.dot(attended[...], wo[:, cols], preferred_element_type=F32).astype(BF16)

            @pl.when(first)
            def _():
                far_copy(item, index).start()
                near_copy(item, index).start()

            @pl.when(second & jnp.logical_not(last))
            def _():
                mem_all(item, index).start()

            @pl.when(second & last)
            def _():
                mem_part(item, index).start()

        @pl.when(second & (item == items - 1))
        def _():
            seg_part(item).start()

    def add_rows(item, cols, start, landed, count):
        slot = item % slots

        @pl.loop(0, count // BAND)
        def _(band):
            span = pl.ds(pl.multiple_of(start + band * BAND, BAND), BAND)
            there = pl.ds(pl.multiple_of(landed + band * BAND, BAND), BAND)
            total = partial[slot, span, cols].astype(F32) + last_sum[item, there, cols].astype(F32)
            rows_in[item, span, cols] = (rows_in[item, span, cols].astype(F32) + total).astype(BF16)

    def finish_memory(item, slot):
        state = state_copies(item)
        for copy in state:
            copy.wait_send()

        @pl.when(item < items - slots)
        def _():
            if slot == 0:
                pl.semaphore_wait(known_sem.at[2], 1)

            @pl.loop(0, CHUNKS)
            def _(index):
                cols = columns(index)
                arrived(last_sum.at[item, pl.ds(0, mem_rows), cols], mem_recv.at[item, index])
                add_rows(item, cols, 0, 0, mem_rows)

                @pl.loop(0, groups // CHUNKS)
                def _(step):
                    piece_copy(slot, index * (groups // CHUNKS) + step).start()

        @pl.when(item >= items - slots)
        def _():
            @pl.loop(0, CHUNKS)
            def _(index):
                cols = columns(index)
                arrived(last_sum.at[item, pl.ds(0, dev_rows), cols], mem_recv.at[item, index])
                add_rows(item, cols, mem_home, 0, dev_rows)

        out_copy(item, 0).start()

    def finish_segment(item):
        arrived(last_sum.at[item, pl.ds(mem_rows, dev_rows)], seg_recv.at[item])

        @pl.loop(0, CHUNKS)
        def _(index):
            add_rows(item, columns(index), seg_home, mem_rows, dev_rows)

        out_copy(item, 1).start()

    @pl.loop(0, items)
    def _(item):
        @pl.when(first & (item == slots))
        def _():
            reorder(0)

        @pl.when(first & (item == slots + 1))
        def _():
            reorder(1)

        @pl.when(second & (item == 1))
        def _():
            finish_memory(item - 1, 0)

        project(item)

        @pl.when(second & (item == items - 1))
        def _():
            seg_part(item - 1).start()

        @pl.when(first & (item == 0))
        def _():
            pl.semaphore_wait(known_sem.at[1], 1)
            tell(2, (1, group, half))

        attend(item)
        emit(item)

        @pl.when(second & (item == items - 1))
        def _():
            finish_memory(item - 1, 0)

        @pl.when(second & (item % slots == 1))
        def _():
            finish_memory(item, 1)

            @pl.when(item < items - slots)
            def _():
                seg_part(item - 1).start()
                seg_part(item).start()

            finish_segment(item - 1)
            finish_segment(item)

    @pl.loop(0, items)
    def _(item):
        last = item >= items - slots

        @pl.when(first)
        def _():
            for source, target in states(item)[:1]:
                arrived(target, state_recv.at[item, 0])
            for source, target in states(item)[1:]:
                arrived(target, state_recv.at[item, 1])
            for index in range(CHUNKS):
                entry_far(item, 1, index).wait_send()
            keep_copy(item).wait_send()

            @pl.when(last)
            def _():
                for index in range(CHUNKS):
                    far_copy(item, index).wait_send()
                    near_copy(item, index).wait_send()

        @pl.when(second)
        def _():
            out_copy(item, 0).wait()
            out_copy(item, 1).wait()

            @pl.when(last)
            def _():
                for index in range(CHUNKS):
                    mem_part(item, index).wait_send()
                seg_part(item).wait_send()

    for slot in range(slots):
        @pl.when(first)
        def _():
            for index in range(CHUNKS):
                entry_far(slot, 0, index).wait_send()
            arrived(picked.at[slot, pl.ds(0, groups - 1)], back_send.at[slot])

        @pl.when(second)
        def _():
            arrived(spread[slot], route_send.at[slot])


def run_window(segments, memory, lengths, routes, gain, w_query, w_key, w_value, w_out):
    rounds, slots, dev_rows, width = segments.shape
    items = rounds * slots
    mem_rows = 2 * dev_rows
    rows = 2 * mem_rows
    groups = width // PIECE
    dma = pltpu.SemaphoreType.DMA
    vmem = pltpu.VMEM
    states = jax.ShapeDtypeStruct((1, rounds, slots, dev_rows, width), BF16)
    q_width, kv_width = w_query.shape[2], w_key.shape[2]
    return pl.pallas_call(
        window_kernel,
        out_shape=(states, states),
        in_specs=[pl.BlockSpec(memory_space=pl.ANY)] * 2
        + [pl.BlockSpec(memory_space=pltpu.SMEM)] * 2
        + [pl.BlockSpec(memory_space=vmem)]
        + [pl.BlockSpec(memory_space=pl.ANY)] * 4,
        out_specs=(pl.BlockSpec(memory_space=pl.ANY), pl.BlockSpec(memory_space=pl.ANY)),
        scratch_shapes=[
            vmem(w_query.shape[1:], BF16),
            vmem(w_key.shape[1:], BF16),
            vmem(w_value.shape[1:], BF16),
            vmem(w_out.shape[1:], BF16),
            vmem((items, rows, width), BF16),
            vmem((slots, rows, width), BF16),
            vmem((slots, rows, width), BF16),
            vmem((slots, rows, width), BF16),
            vmem((items, mem_rows + dev_rows, width), BF16),
            vmem((rows, width // CHUNKS), BF16),
            vmem((rows, 128), F32),
            vmem((rows, q_width), F32),
            vmem((rows, kv_width), F32),
            vmem((rows, kv_width), F32),
            vmem((rows, q_width), BF16),
            vmem((rows, kv_width), BF16),
            vmem((rows, kv_width), BF16),
            vmem((rows, q_width), BF16),
            vmem((groups, mem_rows, PIECE), BF16),
            vmem((groups, mem_rows, PIECE), BF16),
            vmem((slots, groups, mem_rows, PIECE), BF16),
            pltpu.SMEM((slots, groups), jnp.int32),
            dma((CHUNKS, 3)),
            dma((CHUNKS,)),
            dma((items, 2)),
            dma((items, 2, CHUNKS)),
            dma((items, 2, CHUNKS)),
            dma((items,)),
            dma((items,)),
            dma((items, CHUNKS)),
            dma((items, CHUNKS)),
            dma((items, CHUNKS)),
            dma((items, CHUNKS)),
            dma((items, CHUNKS)),
            dma((items, CHUNKS)),
            dma((items,)),
            dma((items,)),
            dma((items, 2)),
            dma((items, 2)),
            dma((items, 2)),
            dma((slots,)),
            dma((slots,)),
            dma((slots,)),
            dma((slots,)),
            pltpu.SemaphoreType.REGULAR((3,)),
        ],
        compiler_params=pltpu.CompilerParams(
            collective_id=0, has_side_effects=True, vmem_limit_bytes=63 * 1024 * 1024
        ),
    )(segments, memory, lengths, routes, gain, w_query, w_key, w_value, w_out)


def place_kernel(mem, seg, mem_out, seg_out, held, in_sem, sem):
    spots = [(kind, rnd, slot) for kind in range(2) for rnd in range(mem.shape[1]) for slot in range(mem.shape[2])]
    ins, outs = [], []
    for kind, rnd, slot in spots:
        source, target = ((mem, mem_out), (seg, seg_out))[kind]
        ins.append(pltpu.make_async_copy(source.at[0, rnd, slot], held.at[kind, rnd, slot], in_sem.at[kind, rnd, slot]))
        outs.append(pltpu.make_async_copy(held.at[kind, rnd, slot], target.at[0, rnd, slot], sem.at[kind, rnd, slot]))
    for copy in ins:
        copy.start()
    for into, out in zip(ins, outs):
        into.wait()
        out.start()
    for out in outs:
        out.wait()


def place(mem, seg):
    anywhere = pl.BlockSpec(memory_space=pl.ANY)
    states = jax.ShapeDtypeStruct(mem.shape, mem.dtype)
    return pl.pallas_call(
        place_kernel,
        out_shape=(states, states),
        in_specs=[anywhere, anywhere],
        out_specs=(anywhere, anywhere),
        scratch_shapes=[
            pltpu.VMEM((2,) + mem.shape[1:], mem.dtype),
            pltpu.SemaphoreType.DMA((2,) + mem.shape[1:3]),
            pltpu.SemaphoreType.DMA((2,) + mem.shape[1:3]),
        ],
        compiler_params=pltpu.CompilerParams(vmem_limit_bytes=63 * 1024 * 1024),
    )(mem, seg)


def per_device(segments, memory_in, seg_lengths, routes, w_query, w_key, value_weight, w_out, norm_gain):
    mem, seg = run_window(
        segments, memory_in, seg_lengths, routes, norm_gain, w_query, w_key, value_weight, w_out)
    return place(mem, seg)


def solution(mesh):
    return jax.shard_map(
        per_device,
        mesh=mesh,
        in_specs=(
            P(None, "dp", "mp", None),
            P("dp", "mp", None),
            P(None, "dp"),
            P(),
            P("phase", None, "mp"),
            P("phase", None, "mp"),
            P("phase", None, "mp"),
            P("phase", "mp", None),
            P("phase", None),
        ),
        out_specs=(P("phase", None, "dp", "mp", None), P("phase", None, "dp", "mp", None)),
        check_vma=False,
    )
```
